32 devices in a mesh: groups: 2 (over y), latent: 8 (over z, x), dp: 2 (over core).
Axes of the slice: x: 2, y: 2, z: 4, core: 2. Of those that a mesh axis runs over, the one named last changes fastest.
Arguments:
- acts: bfloat16 [128, 1792], P(('groups', 'latent', 'dp')), parts along dimension 0, may hold values from -6 to 6
- w_enc: bfloat16 [3584, 65536], P(('groups', 'dp'), 'latent'), parts along dimension 0, may hold values from -0.125 to 0.125
- b_enc: float32 [131072], P(('groups', 'latent')), parts along dimension 0, may hold values from -1.5 to -0.5
- w_dec: bfloat16 [131072, 1792], P(('groups', 'latent'), 'dp'), parts along dimension 0, may hold values from -0.0625 to 0.0625
- dec_m: bfloat16 [131072, 1792], P(('groups', 'latent'), 'dp'), parts along dimension 0, may hold values from -0.03125 to 0.03125
- dec_v: bfloat16 [131072, 1792], P(('groups', 'latent'), 'dp'), parts along dimension 0, may hold values from 9.9651515e-08 to 9.983778e-07
Outputs:
- dec_step: bfloat16 [131072, 1792], P(('groups', 'latent'), 'dp'), parts along dimension 0
The draws below stay inside these ranges and needn't reach their ends.
There are 2 independent parts, one for each index of `groups`. The reference program is written for one: setup_inputs(seed, part) draws one part's arguments, and reference() takes and returns one part's arrays. A program takes and returns all parts, laid end to end along the dimension named above; each array names one. Nothing has to cross between parts.
All inputs are finite; a program needn't handle non-finite values.
Results may differ from the reference program's by a relative error of at most 0.0072.
Values may be sent and summed in bfloat16 or wider, within the bound.
No kernel may reach another device: no remote copies, remote signals or barrier semaphores. Data moves between devices by JAX's collectives and lax.ppermute only.
A program may use at most 256 MiB of HBM per device.

```python
import math
import jax
import jax.numpy as jnp
from jax import lax

D = 1792
LAT = 65536
TOKENS = 64


def block_scale(stream_key, shape, split, smallest, high):
    level = 1.0
    for dim, shards_of in split:
        heights = jax.random.uniform(jax.random.fold_in(jax.random.fold_in(stream_key, 6), dim), (shards_of,), jnp.float32, smallest / len(split), high / len(split))
        level = level * jnp.repeat(jnp.exp(heights), shape[dim] // shards_of).reshape((-1,) + (1,) * (len(shape) - 1 - dim))
    return level


def scatter_about(key, shape, scale, bound, pieces=(), held_as=jnp.bfloat16):
    level = block_scale(key, shape, pieces, -0.22, 0.18) if pieces else 1.0
    entries = jax.random.normal(key, shape, jnp.float32) * scale * level
    return jnp.minimum(jnp.maximum(entries, -bound), bound).astype(held_as)


def setup_inputs(seed: int = 0, part: int = 0) -> dict:
    arg_keys = jax.random.split(jax.random.key(seed), 7)
    own_keys = jax.random.split(jax.random.fold_in(arg_keys[6], part), 7)
    acts = scatter_about(own_keys[0], (TOKENS, D), 1.0, 6.0, ((0, 16),))
    w_enc = scatter_about(own_keys[1], (D, LAT), D ** -0.5, 0.125, ((0, 2), (1, 8)))
    b_enc = jnp.clip(-1.5 + 1.0 * jax.random.uniform(own_keys[2], (LAT,), jnp.float32) ** block_scale(own_keys[2], (LAT,), ((0, 8),), -0.2, 0.2), -1.5, -0.5)
    w_dec = scatter_about(own_keys[3], (LAT, D), (LAT // 8) ** -0.5, 0.0625, ((0, 8), (1, 2)))
    dec_m = scatter_about(own_keys[4], (LAT, D), 0.002, 0.03125, ((0, 8), (1, 2)))
    dec_v = jnp.clip(jnp.exp(math.log(9.98377799987793e-07) - 2.3044525 * jax.random.uniform(own_keys[5], (LAT, D), jnp.float32) ** block_scale(own_keys[5], (LAT, D), ((0, 8), (1, 2)), -0.2, 0.2)), 9.96515154838562e-08, 9.98377799987793e-07).astype(jnp.bfloat16)
    return {"acts": acts, "w_enc": w_enc, "b_enc": b_enc, "w_dec": w_dec, "dec_m": dec_m, "dec_v": dec_v}


def reference(acts, w_enc, b_enc, w_dec, dec_m, dec_v):
    pre = jnp.dot(acts, w_enc, preferred_element_type=jnp.float32) + b_enc
    codes = jnp.maximum(pre, 0.0).astype(jnp.bfloat16)
    recon = jnp.dot(codes, w_dec, preferred_element_type=jnp.float32)
    error = (recon - acts.astype(jnp.float32)).astype(jnp.bfloat16)
    grad = lax.dot_general(codes, error, (((0,), (0,)), ((), ())), preferred_element_type=jnp.float32) / TOKENS
    moment1 = 0.9 * dec_m.astype(jnp.float32) + 0.1 * grad
    moment2 = 0.999 * dec_v.astype(jnp.float32) + 0.001 * grad * grad
    first = moment1 / (1.0 - 0.9 ** 10)
    second = moment2 / (1.0 - 0.999 ** 10)
    return (first / (jnp.sqrt(second) + 1e-08)).astype(jnp.bfloat16)
```

```python
import functools

import jax
import jax.numpy as jnp
from jax import lax
from jax.experimental import pallas as pl
from jax.experimental.pallas import tpu as pltpu
from jax.sharding import PartitionSpec as P

MIB = 1 << 20
WHOLE = pl.BlockSpec(memory_space=pltpu.VMEM)
DIRECT = 8


def swap(value, axis, mask):
    n = lax.axis_size(axis)
    return lax.ppermute(value, axis, [(i, i ^ mask) for i in range(n)])


def params(mib):
    return pltpu.CompilerParams(vmem_limit_bytes=mib * MIB)


def resident(value):
    return pltpu.with_memory_space_constraint(value, pltpu.VMEM)


def pair_kernel(mine, theirs, out):
    half = out.shape[1]
    rows = mine.shape[0]
    side = lax.axis_index("dp")

    def write(first, second, at):
        both = [first[:, at : at + half], second[:, at : at + half]]
        out[...] = jnp.concatenate([b.astype(jnp.float32) for b in both]).astype(out.dtype)

    @pl.when(side == 0)
    def _():
        write(mine, theirs, 0)

    @pl.when(side == 1)
    def _():
        write(theirs, mine, half)


def pair_rows(acts):
    theirs = swap(acts, "dp", 1)
    return pl.pallas_call(
        pair_kernel,
        out_shape=jax.ShapeDtypeStruct((2 * acts.shape[0], acts.shape[1] // 2), acts.dtype),
        in_specs=[WHOLE, WHOLE],
        out_specs=WHOLE,
        compiler_params=params(4),
    )(acts, theirs)


def spread(block):
    n = lax.axis_size("latent")
    if n > DIRECT:
        return [lax.all_gather(block, "latent", axis=0, tiled=True)]
    return [block] + [swap(block, "latent", j) for j in range(1, n)]


def stack(refs):
    if len(refs) == 1:
        return refs[0][...]
    return jnp.concatenate([r[...].astype(jnp.float32) for r in refs]).astype(refs[0].dtype)


def encode_kernel(chunk, *refs):
    *rows_refs, w, out = refs
    rows = stack(rows_refs)

    @pl.loop(0, out.shape[1] // chunk)
    def _(i):
        at = pl.ds(pl.multiple_of(i * chunk, chunk), chunk)
        out[:, at] = jnp.dot(rows, w[:, at], preferred_element_type=jnp.float32)


def encode(blocks, w_enc):
    tokens = sum(b.shape[0] for b in blocks)
    lat = w_enc.shape[1]
    return pl.pallas_call(
        functools.partial(encode_kernel, min(512, lat)),
        out_shape=jax.ShapeDtypeStruct((tokens, lat), jnp.float32),
        in_specs=[WHOLE] * (len(blocks) + 1),
        out_specs=WHOLE,
        compiler_params=params(8),
    )(*blocks, resident(w_enc))


def decode_kernel(chunk, mine, theirs, bias, w, codes, *out):
    tokens, lat = mine.shape
    total = jnp.zeros((tokens, w.shape[1]), jnp.float32)

    def step(i, total):
        at = pl.ds(pl.multiple_of(i * chunk, chunk), chunk)
        pre = mine[:, at] + theirs[:, at] + bias[:, at]
        block = jnp.maximum(pre, 0.0).astype(jnp.bfloat16)
        codes[:, at] = block
        return total + jnp.dot(block, w[at, :], preferred_element_type=jnp.float32)

    total = lax.fori_loop(0, lat // chunk, step, total)
    rows = out[0].shape[0]
    for j, ref in enumerate(out):
        ref[...] = total[j * rows : (j + 1) * rows]


def decode(mine, theirs, bias, w_dec, parts):
    tokens, lat = mine.shape
    half = w_dec.shape[1]
    codes, *sums = pl.pallas_call(
        functools.partial(decode_kernel, min(512, lat)),
        out_shape=[jax.ShapeDtypeStruct((tokens, lat), jnp.bfloat16)]
        + [jax.ShapeDtypeStruct((tokens // parts, half), jnp.float32)] * parts,
        in_specs=[WHOLE] * 4,
        out_specs=[WHOLE] * (1 + parts),
        compiler_params=params(8),
    )(mine, theirs, bias.reshape(1, lat), resident(w_dec))
    return codes, sums


def error_kernel(*refs):
    *sums, rows, out = refs
    total = sums[0][...]
    for ref in sums[1:]:
        total = total + ref[...]
    out[...] = (total - rows[...].astype(jnp.float32)).astype(out.dtype)


def own_error(sums, rows):
    return pl.pallas_call(
        error_kernel,
        out_shape=jax.ShapeDtypeStruct(rows.shape, rows.dtype),
        in_specs=[WHOLE] * (len(sums) + 1),
        out_specs=WHOLE,
        compiler_params=params(4),
    )(*sums, rows)


def reduce_rows(sums):
    n = lax.axis_size("latent")
    if n > DIRECT:
        return [lax.psum_scatter(sums[0], "latent", scatter_dimension=0, tiled=True)]
    return [sums[0]] + [swap(sums[j], "latent", j) for j in range(1, n)]


def adam_kernel(total_rows, codes, m, v, *refs):
    *err_refs, out = refs
    err = stack(err_refs)
    grad = lax.dot_general(
        codes[...], err, (((0,), (0,)), ((), ())), preferred_element_type=jnp.float32
    ) / total_rows
    moment1 = 0.9 * m[...].astype(jnp.float32) + 0.1 * grad
    moment2 = 0.999 * v[...].astype(jnp.float32) + 0.001 * grad * grad
    first = moment1 / (1.0 - 0.9**10)
    second = moment2 / (1.0 - 0.999**10)
    out[...] = (first / (jnp.sqrt(second) + 1e-8)).astype(out.dtype)


def adam(codes, m, v, errs):
    tokens, lat = codes.shape
    half = m.shape[1]
    rows = min(256, lat)
    slab = pl.BlockSpec((rows, half), lambda i: (i, 0))
    return pl.pallas_call(
        functools.partial(adam_kernel, tokens),
        grid=(lat // rows,),
        out_shape=jax.ShapeDtypeStruct(m.shape, jnp.bfloat16),
        in_specs=[pl.BlockSpec((tokens, rows), lambda i: (0, i)), slab, slab] + [WHOLE] * len(errs),
        out_specs=slab,
        compiler_params=params(16),
    )(codes, m, v, *errs)


def per_device(acts, w_enc, b_enc, w_dec, dec_m, dec_v):
    own = pair_rows(acts)
    blocks = spread(own)
    mine = encode(blocks, w_enc)
    theirs = swap(mine, "dp", 1)
    codes, sums = decode(mine, theirs, b_enc, w_dec, len(blocks))
    err = own_error(reduce_rows(sums), own)
    return adam(codes, dec_m, dec_v, spread(err))


def solution(mesh):
    in_specs = (
        P(("groups", "latent", "dp"), None),
        P(("groups", "dp"), "latent"),
        P(("groups", "latent")),
        P(("groups", "latent"), "dp"),
        P(("groups", "latent"), "dp"),
        P(("groups", "latent"), "dp"),
    )
    out_specs = P(("groups", "latent"), "dp")
    return jax.shard_map(
        per_device, mesh=mesh, in_specs=in_specs, out_specs=out_specs, check_vma=False
    )
```

```python
import functools

import jax
import jax.numpy as jnp
from jax import lax
from jax.experimental import pallas as pl
from jax.experimental.pallas import tpu as pltpu
from jax.sharding import PartitionSpec as P

MIB = 1 << 20
WHOLE = pl.BlockSpec(memory_space=pltpu.VMEM)
DIRECT = 8


def swap(value, axis, mask):
    n = lax.axis_size(axis)
    return lax.ppermute(value, axis, [(i, i ^ mask) for i in range(n)])


def params(mib):
    return pltpu.CompilerParams(vmem_limit_bytes=mib * MIB)


def waits(mib):
    return pl.CostEstimate(flops=mib * 350_000_000, bytes_accessed=mib * MIB, transcendentals=0)


def resident(value):
    return pltpu.with_memory_space_constraint(value, pltpu.VMEM)


def pair_kernel(mine, theirs, own, out):
    half = out.shape[-1]
    side = lax.axis_index("dp")

    def write(first, second, at):
        both = [first[:, at : at + half], second[:, at : at + half]]
        rows = jnp.concatenate([b.astype(jnp.float32) for b in both]).astype(out.dtype)
        own[...] = rows
        for i in range(out.shape[0]):
            out[i] = rows

    @pl.when(side == 0)
    def _():
        write(mine, theirs, 0)

    @pl.when(side == 1)
    def _():
        write(theirs, mine, half)


def pair_rows(acts, copies):
    theirs = swap(acts, "dp", 1)
    shape = (2 * acts.shape[0], acts.shape[1] // 2)
    return pl.pallas_call(
        pair_kernel,
        out_shape=[
            jax.ShapeDtypeStruct(shape, acts.dtype),
            jax.ShapeDtypeStruct((copies, *shape), acts.dtype),
        ],
        in_specs=[WHOLE, WHOLE],
        out_specs=[WHOLE, WHOLE],
        cost_estimate=waits(6),
        compiler_params=params(4),
    )(acts, theirs)


def peers(n):
    order, mask = [0], n // 2
    while mask:
        order += [j ^ mask for j in order]
        mask //= 2
    return order


def order_kernel(blocks, out):
    me = lax.axis_index("latent")
    parts = [blocks[me ^ j] for j in peers(blocks.shape[0])]
    out[...] = jnp.concatenate([p.astype(jnp.float32) for p in parts]).astype(out.dtype)


def join_kernel(a, b, out):
    both = [a[...], b[...]]
    out[...] = jnp.concatenate([x.astype(jnp.float32) for x in both]).astype(out.dtype)


def join(a, b):
    return pl.pallas_call(
        join_kernel,
        out_shape=jax.ShapeDtypeStruct((a.shape[0] + b.shape[0], a.shape[1]), a.dtype),
        in_specs=[WHOLE, WHOLE],
        out_specs=WHOLE,
        cost_estimate=waits(4),
        compiler_params=params(4),
    )(a, b)


def gather_rows(acts):
    n = lax.axis_size("latent")
    if n > DIRECT:
        own, _ = pair_rows(acts, 1)
        return lax.all_gather(own, "latent", axis=0, tiled=True), own
    own, copies = pair_rows(acts, n)
    blocks = lax.all_to_all(copies, "latent", 0, 0, tiled=True)
    rows = pl.pallas_call(
        order_kernel,
        out_shape=jax.ShapeDtypeStruct((n * copies.shape[1], copies.shape[2]), acts.dtype),
        in_specs=[WHOLE],
        out_specs=WHOLE,
        cost_estimate=waits(6),
        compiler_params=params(4),
    )(blocks)
    return rows, own


def spread(block):
    n = lax.axis_size("latent")
    if n > DIRECT:
        return lax.all_gather(block, "latent", axis=0, tiled=True)
    mask = n // 2
    while mask:
        block = join(block, swap(block, "latent", mask))
        mask //= 2
    return block


def encode_kernel(chunk, rows_ref, w, out):
    rows = rows_ref[...]

    @pl.loop(0, out.shape[1] // chunk)
    def _(i):
        at = pl.ds(pl.multiple_of(i * chunk, chunk), chunk)
        out[:, at] = jnp.dot(rows, w[:, at], preferred_element_type=jnp.float32)


def encode(rows, w_enc):
    tokens, lat = rows.shape[0], w_enc.shape[1]
    return pl.pallas_call(
        functools.partial(encode_kernel, min(512, lat)),
        out_shape=jax.ShapeDtypeStruct((tokens, lat), jnp.float32),
        in_specs=[WHOLE] * 2,
        out_specs=WHOLE,
        cost_estimate=waits(14),
        compiler_params=params(8),
    )(rows, resident(w_enc))


def decode_kernel(chunk, mine, theirs, bias, w, codes, *out):
    tokens, lat = mine.shape
    total = jnp.zeros((tokens, w.shape[1]), jnp.float32)

    def step(i, total):
        at = pl.ds(pl.multiple_of(i * chunk, chunk), chunk)
        pre = mine[:, at] + theirs[:, at] + bias[:, at]
        block = jnp.maximum(pre, 0.0).astype(jnp.bfloat16)
        codes[:, at] = block
        return total + jnp.dot(block, w[at, :], preferred_element_type=jnp.float32)

    total = lax.fori_loop(0, lat // chunk, step, total)
    rows = tokens // len(out)
    for j, ref in enumerate(out):
        ref[...] = total[j * rows : (j + 1) * rows]


def decode(mine, theirs, bias, w_dec, parts):
    tokens, lat = mine.shape
    half = w_dec.shape[1]
    codes, *sums = pl.pallas_call(
        functools.partial(decode_kernel, min(512, lat)),
        out_shape=[jax.ShapeDtypeStruct((tokens, lat), jnp.bfloat16)]
        + [jax.ShapeDtypeStruct((tokens // parts, half), jnp.float32)] * parts,
        in_specs=[WHOLE] * 4,
        out_specs=[WHOLE] * (1 + parts),
        cost_estimate=waits(14),
        compiler_params=params(8),
    )(mine, theirs, bias.reshape(1, lat), resident(w_dec))
    return codes, sums


def turn_kernel(chunk, codes, out):
    @pl.loop(0, out.shape[0] // chunk)
    def _(i):
        at = pl.ds(pl.multiple_of(i * chunk, chunk), chunk)
        out[at, :] = codes[:, at].astype(jnp.float32).T.astype(out.dtype)


def turn(codes):
    tokens, lat = codes.shape
    return pl.pallas_call(
        functools.partial(turn_kernel, min(512, lat)),
        out_shape=jax.ShapeDtypeStruct((lat, tokens), codes.dtype),
        in_specs=[WHOLE],
        out_specs=WHOLE,
        cost_estimate=waits(4),
        compiler_params=params(8),
    )(codes)


def halve_kernel(a, b, keep, send):
    total = a[...] + b[...]
    half = keep.shape[0]
    keep[...] = total[:half]
    send[...] = total[half:]


def halve(a, b):
    rows, half = a.shape
    return pl.pallas_call(
        halve_kernel,
        out_shape=[jax.ShapeDtypeStruct((rows // 2, half), a.dtype)] * 2,
        in_specs=[WHOLE] * 2,
        out_specs=[WHOLE] * 2,
        cost_estimate=waits(4),
        compiler_params=params(4),
    )(a, b)


def error_kernel(*refs):
    *sums, rows, out = refs
    total = sums[0][...]
    for ref in sums[1:]:
        total = total + ref[...]
    out[...] = (total - rows[...].astype(jnp.float32)).astype(out.dtype)


def own_error(sums, rows):
    return pl.pallas_call(
        error_kernel,
        out_shape=jax.ShapeDtypeStruct(rows.shape, rows.dtype),
        in_specs=[WHOLE] * (len(sums) + 1),
        out_specs=WHOLE,
        cost_estimate=waits(4),
        compiler_params=params(4),
    )(*sums, rows)


def reduce_rows(sums):
    n = lax.axis_size("latent")
    if n > DIRECT:
        return [lax.psum_scatter(sums[0], "latent", scatter_dimension=0, tiled=True)]
    keep, send = sums
    mask = 1
    while mask < n // 2:
        keep, send = halve(keep, swap(send, "latent", mask))
        mask *= 2
    return [keep, swap(send, "latent", mask)]


def adam_kernel(codes_t, err, m, v, out, *products):
    tokens = codes_t.shape[1]
    b = 0.1 / (1.0 - 0.9**10) / tokens
    a = 0.9 / (1.0 - 0.9**10) / b
    p = 0.999 / (1.0 - 0.999**10) / b**2
    q = 0.001 / (1.0 - 0.999**10) / tokens**2 / b**2
    eps = 1e-8 / b
    i, last = pl.program_id(0), pl.num_programs(0) - 1
    rows = out.shape[0]
    part = rows // len(products)

    def multiply(block, k):
        at = pl.ds(pl.multiple_of(block * rows + k * part, part), part)
        products[k][...] = jnp.dot(codes_t[at, :], err[...], preferred_element_type=jnp.float32)

    @pl.when(i == 0)
    def _():
        multiply(0, 0)

    for k in range(len(products)):
        if k + 1 < len(products):
            multiply(i, k + 1)
        else:
            multiply(jnp.minimum(i + 1, last), 0)
        for r in range(0, part, 16):
            at = pl.ds(pl.multiple_of(i * rows + k * part + r, 16), 16)
            c = products[k][r : r + 16, :]
            first = m[at, :].astype(jnp.float32) * a + c
            second = v[at, :].astype(jnp.float32) * p + (c * c) * q
            root = second * lax.rsqrt(second)
            step = first * pl.reciprocal(root + eps, approx=True)
            out[k * part + r : k * part + r + 16, :] = step.astype(out.dtype)


def adam(codes_t, err, m, v):
    lat, half = m.shape
    rows = min(512, lat)
    parts = 4
    return pl.pallas_call(
        adam_kernel,
        grid=(lat // rows,),
        out_shape=jax.ShapeDtypeStruct(m.shape, jnp.bfloat16),
        in_specs=[WHOLE] * 4,
        out_specs=pl.BlockSpec((rows, half), lambda i: (i, 0)),
        scratch_shapes=[pltpu.VMEM((rows // parts, half), jnp.float32)] * parts,
        compiler_params=params(8),
    )(codes_t, err, resident(m), resident(v))


def per_device(acts, w_enc, b_enc, w_dec, dec_m, dec_v):
    rows, own = gather_rows(acts)
    mine = encode(rows, w_enc)
    theirs = swap(mine, "dp", 1)
    direct = lax.axis_size("latent") <= DIRECT
    codes, sums = decode(mine, theirs, b_enc, w_dec, 2 if direct else 1)
    codes_t = turn(codes)
    err = spread(own_error(reduce_rows(sums), own))
    return adam(codes_t, err, dec_m, dec_v)


def solution(mesh):
    in_specs = (
        P(("groups", "latent", "dp"), None),
        P(("groups", "dp"), "latent"),
        P(("groups", "latent")),
        P(("groups", "latent"), "dp"),
        P(("groups", "latent"), "dp"),
        P(("groups", "latent"), "dp"),
    )
    out_specs = P(("groups", "latent"), "dp")
    return jax.shard_map(
        per_device, mesh=mesh, in_specs=in_specs, out_specs=out_specs, check_vma=False
    )
```

```python
import functools

import jax
import jax.numpy as jnp
from jax import lax
from jax.experimental import pallas as pl
from jax.experimental.pallas import tpu as pltpu
from jax.sharding import PartitionSpec as P

MIB = 1 << 20
WHOLE = pl.BlockSpec(memory_space=pltpu.VMEM)
DIRECT = 8


def swap(value, axis, mask):
    n = lax.axis_size(axis)
    return lax.ppermute(value, axis, [(i, i ^ mask) for i in range(n)])


def params(mib):
    return pltpu.CompilerParams(vmem_limit_bytes=mib * MIB)


def waits(mib):
    return pl.CostEstimate(flops=mib * 350_000_000, bytes_accessed=mib * MIB, transcendentals=0)


def resident(value):
    return pltpu.with_memory_space_constraint(value, pltpu.VMEM)


def far_masks():
    return range(2, lax.axis_size("latent"), 2)


def stack(refs):
    return jnp.concatenate([r[...].astype(jnp.float32) for r in refs]).astype(refs[0].dtype)


def near_kernel(*refs):
    *rows, out = refs
    half = out.shape[1]
    side = lax.axis_index("dp")

    def write(order, at):
        picked = [rows[i][:, at : at + half].astype(jnp.float32) for i in order]
        out[...] = jnp.concatenate(picked).astype(out.dtype)

    pairs = range(0, len(rows), 2)

    @pl.when(side == 0)
    def _():
        write([i + c for i in pairs for c in (0, 1)], 0)

    @pl.when(side == 1)
    def _():
        write([i + c for i in pairs for c in (1, 0)], half)


def near_rows(acts, near):
    axes = ("latent", "dp")
    rows = [acts] + [swap(acts, axes, mask) for mask in range(1, 2 * near)]
    return pl.pallas_call(
        near_kernel,
        out_shape=jax.ShapeDtypeStruct((len(rows) * acts.shape[0], acts.shape[1] // 2), acts.dtype),
        in_specs=[WHOLE] * len(rows),
        out_specs=WHOLE,
        cost_estimate=waits(14),
        compiler_params=params(4),
    )(*rows)


def spread(block):
    if lax.axis_size("latent") > DIRECT:
        return [lax.all_gather(block, "latent", axis=0, tiled=True)]
    return [block] + [swap(block, "latent", mask) for mask in far_masks()]


def encode_kernel(first, chunk, *refs):
    *rows_refs, w, out = refs
    rows = stack(rows_refs)

    @pl.loop(0, out.shape[1] // chunk)
    def _(i):
        at = pl.multiple_of(i * chunk, chunk)
        out[:, pl.ds(at, chunk)] = jnp.dot(
            rows, w[:, pl.ds(first + at, chunk)], preferred_element_type=jnp.float32
        )


def encode(blocks, w_enc, first, lat):
    tokens = sum(b.shape[0] for b in blocks)
    return pl.pallas_call(
        functools.partial(encode_kernel, first, min(512, lat)),
        out_shape=jax.ShapeDtypeStruct((tokens, lat), jnp.float32),
        in_specs=[WHOLE] * (len(blocks) + 1),
        out_specs=WHOLE,
        cost_estimate=waits(7),
        compiler_params=params(8),
    )(*blocks, resident(w_enc))


def decode_kernel(first, chunk, given, mine, theirs, bias, w, *refs):
    codes, *out = refs[given:]
    tokens, lat = mine.shape
    total = refs[0][...] if given else jnp.zeros((tokens, w.shape[1]), jnp.float32)

    def step(i, total):
        at = pl.multiple_of(i * chunk, chunk)
        part, whole = pl.ds(at, chunk), pl.ds(first + at, chunk)
        pre = mine[:, part] + theirs[:, part] + bias[:, whole]
        block = jnp.maximum(pre, 0.0).astype(jnp.bfloat16)
        codes[:, part] = block
        return total + jnp.dot(block, w[whole, :], preferred_element_type=jnp.float32)

    total = lax.fori_loop(0, lat // chunk, step, total)
    rows = tokens // len(out)
    for j, ref in enumerate(out):
        ref[...] = total[j * rows : (j + 1) * rows]


def decode(mine, theirs, bias, w_dec, first, given, parts):
    tokens, lat = mine.shape
    half = w_dec.shape[1]
    codes, *sums = pl.pallas_call(
        functools.partial(decode_kernel, first, min(512, lat), len(given)),
        out_shape=[jax.ShapeDtypeStruct((tokens, lat), jnp.bfloat16)]
        + [jax.ShapeDtypeStruct((tokens // parts, half), jnp.float32)] * parts,
        in_specs=[WHOLE] * (4 + len(given)),
        out_specs=[WHOLE] * (1 + parts),
        cost_estimate=waits(7),
        compiler_params=params(8),
    )(mine, theirs, bias.reshape(1, -1), resident(w_dec), *given)
    return codes, sums


def turn_kernel(chunk, *refs):
    *codes, out = refs
    for k, ref in enumerate(codes):
        lat = ref.shape[1]

        @pl.loop(0, lat // chunk)
        def _(i):
            at = pl.multiple_of(i * chunk, chunk)
            block = ref[:, pl.ds(at, chunk)].astype(jnp.float32).T
            out[pl.ds(k * lat + at, chunk), :] = block.astype(out.dtype)


def turn(*codes):
    tokens, lat = codes[0].shape
    return pl.pallas_call(
        functools.partial(turn_kernel, min(512, lat)),
        out_shape=jax.ShapeDtypeStruct((len(codes) * lat, tokens), codes[0].dtype),
        in_specs=[WHOLE] * len(codes),
        out_specs=WHOLE,
        cost_estimate=waits(4),
        compiler_params=params(8),
    )(*codes)


def sum_kernel(*refs):
    *terms, out = refs
    total = terms[0][...]
    for ref in terms[1:]:
        total = total + ref[...]
    out[...] = total


def add_up(terms):
    return pl.pallas_call(
        sum_kernel,
        out_shape=jax.ShapeDtypeStruct(terms[0].shape, jnp.float32),
        in_specs=[WHOLE] * len(terms),
        out_specs=WHOLE,
        cost_estimate=waits(8),
        compiler_params=params(4),
    )(*terms)


def error_kernel(total, rows, *refs):
    *near, out = refs
    total = total[...]
    for ref in near:
        half = ref.shape[0] // 2
        total = total + jnp.concatenate([ref[half:], ref[:half]])
    out[...] = (total - rows[...].astype(jnp.float32)).astype(out.dtype)


def error(total, near, rows):
    return pl.pallas_call(
        error_kernel,
        out_shape=jax.ShapeDtypeStruct(rows.shape, rows.dtype),
        in_specs=[WHOLE] * (2 + len(near)),
        out_specs=WHOLE,
        cost_estimate=waits(8),
        compiler_params=params(4),
    )(total, rows, *near)


def reduce_rows(sums):
    if lax.axis_size("latent") > DIRECT:
        return lax.psum_scatter(sums[0], "latent", scatter_dimension=0, tiled=True), []
    terms = [sums[0]] + [swap(s, "latent", mask) for s, mask in zip(sums[1:], far_masks())]
    total = add_up(terms)
    return total, [swap(total, "latent", 1)]


def adam_kernel(blocks, codes_t, m, v, *refs):
    err_refs, out, products, err = refs[:blocks], refs[blocks], refs[blocks + 1 : -1], refs[-1]
    tokens = codes_t.shape[1]
    b = 0.1 / (1.0 - 0.9**10) / tokens
    a = 0.9 / (1.0 - 0.9**10) / b
    p = 0.999 / (1.0 - 0.999**10) / b**2
    q = 0.001 / (1.0 - 0.999**10) / tokens**2 / b**2
    eps = jnp.float32(1e-8 / b)
    i, last = pl.program_id(0), pl.num_programs(0) - 1
    rows = out.shape[0]
    part = rows // len(products)

    def multiply(block, k):
        at = pl.ds(pl.multiple_of(block * rows + k * part, part), part)
        products[k][...] = jnp.dot(codes_t[at, :], err[...], preferred_element_type=jnp.float32)

    @pl.when(i == 0)
    def _():
        err[...] = stack(err_refs)
        multiply(0, 0)

    for k in range(len(products)):
        if k + 1 < len(products):
            multiply(i, k + 1)
        else:
            multiply(jnp.minimum(i + 1, last), 0)
        for r in range(0, part, 16):
            at = pl.ds(pl.multiple_of(i * rows + k * part + r, 16), 16)
            c = products[k][r : r + 16, :]
            first = m[at, :].astype(jnp.float32) * a + c
            second = v[at, :].astype(jnp.float32) * p + (c * c) * q
            second = second.astype(out.dtype)
            root = second * lax.rsqrt(second)
            step = first.astype(out.dtype) * pl.reciprocal(root + eps.astype(out.dtype), approx=True)
            out[k * part + r : k * part + r + 16, :] = step


def adam(codes_t, blocks, m, v):
    lat, half = m.shape
    rows = min(512, lat)
    parts = 4
    return pl.pallas_call(
        functools.partial(adam_kernel, len(blocks)),
        grid=(lat // rows,),
        out_shape=jax.ShapeDtypeStruct(m.shape, jnp.bfloat16),
        in_specs=[WHOLE] * (3 + len(blocks)),
        out_specs=pl.BlockSpec((rows, half), lambda i: (i, 0)),
        scratch_shapes=[pltpu.VMEM((rows // parts, half), jnp.float32)] * parts
        + [pltpu.VMEM((codes_t.shape[1], half), jnp.bfloat16)],
        compiler_params=params(8),
    )(codes_t, resident(m), resident(v), *blocks)


def per_device(acts, w_enc, b_enc, w_dec, dec_m, dec_v):
    direct = lax.axis_size("latent") <= DIRECT
    rows = near_rows(acts, 2 if direct else 1)
    blocks = spread(rows)
    part = w_enc.shape[1] // 2
    mine = [encode(blocks, w_enc, k * part, part) for k in range(2)]
    theirs = [swap(x, "dp", 1) for x in mine]
    codes, sums = [None, None], []
    for k in range(2):
        codes[k], sums = decode(
            mine[k], theirs[k], b_enc, w_dec, k * part, sums, len(blocks) if k else 1
        )
    codes_t = turn(*codes)
    total, near = reduce_rows(sums)
    err = spread(error(total, near, rows))
    return adam(codes_t, err, dec_m, dec_v)


def solution(mesh):
    in_specs = (
        P(("groups", "latent", "dp"), None),
        P(("groups", "dp"), "latent"),
        P(("groups", "latent")),
        P(("groups", "latent"), "dp"),
        P(("groups", "latent"), "dp"),
        P(("groups", "latent"), "dp"),
    )
    out_specs = P(("groups", "latent"), "dp")
    return jax.shard_map(
        per_device, mesh=mesh, in_specs=in_specs, out_specs=out_specs, check_vma=False
    )
```

```python
import functools

import jax
import jax.numpy as jnp
from jax import lax
from jax.experimental import pallas as pl
from jax.experimental.pallas import tpu as pltpu
from jax.sharding import PartitionSpec as P

MIB = 1 << 20
WHOLE = pl.BlockSpec(memory_space=pltpu.VMEM)
DIRECT = 8


def swap(value, axis, mask):
    n = lax.axis_size(axis)
    return lax.ppermute(value, axis, [(i, i ^ mask) for i in range(n)])


def params(mib):
    return pltpu.CompilerParams(vmem_limit_bytes=mib * MIB)


def waits(mib):
    return pl.CostEstimate(flops=mib * 350_000_000, bytes_accessed=mib * MIB, transcendentals=0)


def resident(value):
    return pltpu.with_memory_space_constraint(value, pltpu.VMEM)


def far_masks():
    return range(2, lax.axis_size("latent"), 2)


def stack(refs):
    return jnp.concatenate([r[...].astype(jnp.float32) for r in refs]).astype(refs[0].dtype)


def near_kernel(*refs):
    *rows, out = refs
    half = out.shape[1]
    side = lax.axis_index("dp")

    def write(order, at):
        picked = [rows[i][:, at : at + half].astype(jnp.float32) for i in order]
        out[...] = jnp.concatenate(picked).astype(out.dtype)

    pairs = range(0, len(rows), 2)

    @pl.when(side == 0)
    def _():
        write([i + c for i in pairs for c in (0, 1)], 0)

    @pl.when(side == 1)
    def _():
        write([i + c for i in pairs for c in (1, 0)], half)


def copy_kernel(x, out):
    out[...] = x[...]


def near_rows(acts, near):
    axes = ("latent", "dp")
    own = pl.pallas_call(
        copy_kernel,
        out_shape=jax.ShapeDtypeStruct(acts.shape, acts.dtype),
        in_specs=[WHOLE],
        out_specs=WHOLE,
        cost_estimate=waits(1),
        compiler_params=params(4),
    )(acts)
    rows = [own] + [swap(acts, axes, mask) for mask in range(1, 2 * near)]
    return pl.pallas_call(
        near_kernel,
        out_shape=jax.ShapeDtypeStruct((len(rows) * acts.shape[0], acts.shape[1] // 2), acts.dtype),
        in_specs=[WHOLE] * len(rows),
        out_specs=WHOLE,
        cost_estimate=waits(14),
        compiler_params=params(4),
    )(*rows)


def spread(block):
    if lax.axis_size("latent") > DIRECT:
        return [lax.all_gather(block, "latent", axis=0, tiled=True)]
    return [block] + [swap(block, "latent", mask) for mask in far_masks()]


def encode_kernel(first, chunk, *refs):
    *rows_refs, w, out = refs
    rows = stack(rows_refs)

    @pl.loop(0, out.shape[1] // chunk)
    def _(i):
        at = pl.multiple_of(i * chunk, chunk)
        out[:, pl.ds(at, chunk)] = jnp.dot(
            rows, w[:, pl.ds(first + at, chunk)], preferred_element_type=jnp.float32
        )


def encode(blocks, w_enc, first, lat):
    tokens = sum(b.shape[0] for b in blocks)
    return pl.pallas_call(
        functools.partial(encode_kernel, first, min(512, lat)),
        out_shape=jax.ShapeDtypeStruct((tokens, lat), jnp.float32),
        in_specs=[WHOLE] * (len(blocks) + 1),
        out_specs=WHOLE,
        cost_estimate=waits(7),
        compiler_params=params(8),
    )(*blocks, resident(w_enc))


def decode_kernel(first, chunk, given, mine, theirs, bias, w, *refs):
    codes, *out = refs[given:]
    tokens, lat = mine.shape
    total = refs[0][...] if given else jnp.zeros((tokens, w.shape[1]), jnp.float32)

    def step(i, total):
        at = pl.multiple_of(i * chunk, chunk)
        part, whole = pl.ds(at, chunk), pl.ds(first + at, chunk)
        pre = mine[:, part] + theirs[:, part] + bias[:, whole]
        block = jnp.maximum(pre, 0.0).astype(jnp.bfloat16)
        codes[:, part] = block
        return total + jnp.dot(block, w[whole, :], preferred_element_type=jnp.float32)

    total = lax.fori_loop(0, lat // chunk, step, total)
    rows = tokens // len(out)
    for j, ref in enumerate(out):
        ref[...] = total[j * rows : (j + 1) * rows].astype(ref.dtype)


def decode(mine, theirs, bias, w_dec, first, given, parts):
    tokens, lat = mine.shape
    half = w_dec.shape[1]
    codes, *sums = pl.pallas_call(
        functools.partial(decode_kernel, first, min(512, lat), len(given)),
        out_shape=[jax.ShapeDtypeStruct((tokens, lat), jnp.bfloat16)]
        + [
            jax.ShapeDtypeStruct((tokens // parts, half), jnp.bfloat16 if j else jnp.float32)
            for j in range(parts)
        ],
        in_specs=[WHOLE] * (4 + len(given)),
        out_specs=[WHOLE] * (1 + parts),
        cost_estimate=waits(7),
        compiler_params=params(8),
    )(mine, theirs, bias.reshape(1, -1), resident(w_dec), *given)
    return codes, sums


def turn_kernel(chunk, *refs):
    *codes, out = refs
    for k, ref in enumerate(codes):
        lat = ref.shape[1]

        @pl.loop(0, lat // chunk)
        def _(i):
            at = pl.multiple_of(i * chunk, chunk)
            block = ref[:, pl.ds(at, chunk)].astype(jnp.float32).T
            out[pl.ds(k * lat + at, chunk), :] = block.astype(out.dtype)


def turn(*codes):
    tokens, lat = codes[0].shape
    return pl.pallas_call(
        functools.partial(turn_kernel, min(512, lat)),
        out_shape=jax.ShapeDtypeStruct((len(codes) * lat, tokens), codes[0].dtype),
        in_specs=[WHOLE] * len(codes),
        out_specs=WHOLE,
        cost_estimate=waits(4),
        compiler_params=params(8),
    )(*codes)


def sum_kernel(own, *refs):
    *terms, out, sent = refs
    total = own[...]
    for ref in terms:
        total = total + ref[...]
    out[...] = total
    sent[...] = total.astype(sent.dtype)


def add_up(terms):
    shape = terms[0].shape
    return pl.pallas_call(
        sum_kernel,
        out_shape=[
            jax.ShapeDtypeStruct(shape, jnp.float32),
            jax.ShapeDtypeStruct(shape, jnp.bfloat16),
        ],
        in_specs=[WHOLE] * len(terms),
        out_specs=[WHOLE] * 2,
        cost_estimate=waits(8),
        compiler_params=params(4),
    )(*terms)


def error_kernel(total, rows, *refs):
    *near, out = refs
    total = total[...]
    for ref in near:
        half = ref.shape[0] // 2
        term = ref[...].astype(jnp.float32)
        total = total + jnp.concatenate([term[half:], term[:half]])
    out[...] = (total - rows[...].astype(jnp.float32)).astype(out.dtype)


def error(total, near, rows):
    return pl.pallas_call(
        error_kernel,
        out_shape=jax.ShapeDtypeStruct(rows.shape, rows.dtype),
        in_specs=[WHOLE] * (2 + len(near)),
        out_specs=WHOLE,
        cost_estimate=waits(8),
        compiler_params=params(4),
    )(total, rows, *near)


def reduce_rows(sums):
    if lax.axis_size("latent") > DIRECT:
        return lax.psum_scatter(sums[0], "latent", scatter_dimension=0, tiled=True), []
    terms = [sums[0]] + [swap(s, "latent", mask) for s, mask in zip(sums[1:], far_masks())]
    total, sent = add_up(terms)
    return total, [swap(sent, "latent", 1)]


def adam_kernel(blocks, codes_t, m, v, *refs):
    err_refs, out, products, err = refs[:blocks], refs[blocks], refs[blocks + 1 : -1], refs[-1]
    tokens = codes_t.shape[1]
    b = 0.1 / (1.0 - 0.9**10) / tokens
    a = 0.9 / (1.0 - 0.9**10) / b
    p = 0.999 / (1.0 - 0.999**10) / b**2
    q = 0.001 / (1.0 - 0.999**10) / tokens**2 / b**2
    eps = 1e-8 / b
    i, last = pl.program_id(0), pl.num_programs(0) - 1
    rows = out.shape[0]
    part = rows // len(products)

    def multiply(block, k):
        at = pl.ds(pl.multiple_of(block * rows + k * part, part), part)
        products[k][...] = jnp.dot(codes_t[at, :], err[...], preferred_element_type=jnp.float32)

    @pl.when(i == 0)
    def _():
        err[...] = stack(err_refs)
        multiply(0, 0)

    for k in range(len(products)):
        if k + 1 < len(products):
            multiply(i, k + 1)
        else:
            multiply(jnp.minimum(i + 1, last), 0)
        for r in range(0, part, 16):
            at = pl.ds(pl.multiple_of(i * rows + k * part + r, 16), 16)
            c = products[k][r : r + 16, :]
            first = m[at, :].astype(jnp.float32) * a + c
            second = v[at, :].astype(jnp.float32) * p + (c * c) * q
            root = second * lax.rsqrt(second)
            step = first * pl.reciprocal(root + eps, approx=True)
            out[k * part + r : k * part + r + 16, :] = step.astype(out.dtype)


def adam(codes_t, blocks, m, v):
    lat, half = m.shape
    rows = min(1024, lat)
    parts = 2
    return pl.pallas_call(
        functools.partial(adam_kernel, len(blocks)),
        grid=(lat // rows,),
        out_shape=jax.ShapeDtypeStruct(m.shape, jnp.bfloat16),
        in_specs=[WHOLE] * (3 + len(blocks)),
        out_specs=pl.BlockSpec((rows, half), lambda i: (i, 0)),
        scratch_shapes=[pltpu.VMEM((rows // parts, half), jnp.float32)] * parts
        + [pltpu.VMEM((codes_t.shape[1], half), jnp.bfloat16)],
        compiler_params=params(12),
    )(codes_t, resident(m), resident(v), *blocks)


def per_device(acts, w_enc, b_enc, w_dec, dec_m, dec_v):
    direct = lax.axis_size("latent") <= DIRECT
    rows = near_rows(acts, 2 if direct else 1)
    blocks = spread(rows)
    part = w_enc.shape[1] // 2
    mine = [encode(blocks, w_enc, k * part, part) for k in range(2)]
    theirs = [swap(x, "dp", 1) for x in mine]
    codes, sums = [None, None], []
    for k in range(2):
        codes[k], sums = decode(
            mine[k], theirs[k], b_enc, w_dec, k * part, sums, len(blocks) if k else 1
        )
    codes_t = turn(*codes)
    total, near = reduce_rows(sums)
    err = spread(error(total, near, rows))
    return adam(codes_t, err, dec_m, dec_v)


def solution(mesh):
    in_specs = (
        P(("groups", "latent", "dp"), None),
        P(("groups", "dp"), "latent"),
        P(("groups", "latent")),
        P(("groups", "latent"), "dp"),
        P(("groups", "latent"), "dp"),
        P(("groups", "latent"), "dp"),
    )
    out_specs = P(("groups", "latent"), "dp")
    return jax.shard_map(
        per_device, mesh=mesh, in_specs=in_specs, out_specs=out_specs, check_vma=False
    )
```

```python
import functools

import jax
import jax.numpy as jnp
from jax import lax
from jax.experimental import pallas as pl
from jax.experimental.pallas import tpu as pltpu
from jax.sharding import PartitionSpec as P

MIB = 1 << 20
WHOLE = pl.BlockSpec(memory_space=pltpu.VMEM)
DIRECT = 8


def swap(value, axis, mask):
    n = lax.axis_size(axis)
    return lax.ppermute(value, axis, [(i, i ^ mask) for i in range(n)])


def params(mib):
    return pltpu.CompilerParams(vmem_limit_bytes=mib * MIB)


def waits(mib):
    return pl.CostEstimate(flops=mib * 350_000_000, bytes_accessed=mib * MIB, transcendentals=0)


def resident(value):
    return pltpu.with_memory_space_constraint(value, pltpu.VMEM)


def far_masks():
    return range(2, lax.axis_size("latent"), 2)


def stack(refs):
    return jnp.concatenate([r[...].astype(jnp.float32) for r in refs]).astype(refs[0].dtype)


def near_kernel(*refs):
    *rows, out = refs
    half = out.shape[1]
    side = lax.axis_index("dp")

    def write(order, at):
        picked = [rows[i][:, at : at + half].astype(jnp.float32) for i in order]
        out[...] = jnp.concatenate(picked).astype(out.dtype)

    pairs = range(0, len(rows), 2)

    @pl.when(side == 0)
    def _():
        write([i + c for i in pairs for c in (0, 1)], 0)

    @pl.when(side == 1)
    def _():
        write([i + c for i in pairs for c in (1, 0)], half)


def copy_kernel(x, out):
    out[...] = x[...]


def near_rows(acts, near):
    axes = ("latent", "dp")
    own = pl.pallas_call(
        copy_kernel,
        out_shape=jax.ShapeDtypeStruct(acts.shape, acts.dtype),
        in_specs=[WHOLE],
        out_specs=WHOLE,
        cost_estimate=waits(1),
        compiler_params=params(4),
    )(acts)
    rows = [own] + [swap(acts, axes, mask) for mask in range(1, 2 * near)]
    return pl.pallas_call(
        near_kernel,
        out_shape=jax.ShapeDtypeStruct((len(rows) * acts.shape[0], acts.shape[1] // 2), acts.dtype),
        in_specs=[WHOLE] * len(rows),
        out_specs=WHOLE,
        cost_estimate=waits(14),
        compiler_params=params(4),
    )(*rows)


def spread(block):
    if lax.axis_size("latent") > DIRECT:
        return [lax.all_gather(block, "latent", axis=0, tiled=True)]
    return [block] + [swap(block, "latent", mask) for mask in far_masks()]


def encode_kernel(first, *refs):
    *rows_refs, w, out = refs
    lat = out.shape[1]
    out[...] = jnp.dot(
        stack(rows_refs), w[:, first : first + lat], preferred_element_type=jnp.float32
    )


def encode(blocks, w_enc, first, lat):
    tokens = sum(b.shape[0] for b in blocks)
    return pl.pallas_call(
        functools.partial(encode_kernel, first),
        out_shape=jax.ShapeDtypeStruct((tokens, lat), jnp.float32),
        in_specs=[WHOLE] * (len(blocks) + 1),
        out_specs=WHOLE,
        cost_estimate=waits(7),
        compiler_params=params(8),
    )(*blocks, resident(w_enc))


def decode_kernel(first, given, mine, theirs, bias, w, *refs):
    codes, *out = refs[given:]
    lat = mine.shape[1]
    pre = mine[...] + theirs[...] + bias[:, first : first + lat]
    block = jnp.maximum(pre, 0.0).astype(jnp.bfloat16)
    codes[...] = block
    total = jnp.dot(block, w[first : first + lat, :], preferred_element_type=jnp.float32)
    if given:
        total = total + refs[0][...]
    if len(out) == 1:
        out[0][...] = total
        return
    own, sent = out
    rows = own.shape[0]
    own[...] = total[:rows]
    far = lax.axis_index("latent") // 2
    for j in range(sent.shape[0]):
        sent[far ^ j] = total[j * rows : (j + 1) * rows].astype(sent.dtype)


def decode(mine, theirs, bias, w_dec, first, given, far):
    tokens, lat = mine.shape
    half = w_dec.shape[1]
    sums = [jax.ShapeDtypeStruct((tokens // far, half), jnp.float32)]
    if far > 1:
        sums.append(jax.ShapeDtypeStruct((far, tokens // far, half), jnp.bfloat16))
    codes, *sums = pl.pallas_call(
        functools.partial(decode_kernel, first, len(given)),
        out_shape=[jax.ShapeDtypeStruct((tokens, lat), jnp.bfloat16)] + sums,
        in_specs=[WHOLE] * (4 + len(given)),
        out_specs=[WHOLE] * (1 + len(sums)),
        cost_estimate=waits(7),
        compiler_params=params(8),
    )(mine, theirs, bias.reshape(1, -1), resident(w_dec), *given)
    return codes, sums


def turn_kernel(chunk, *refs):
    *codes, out = refs
    for k, ref in enumerate(codes):
        lat = ref.shape[1]

        @pl.loop(0, lat // chunk)
        def _(i):
            at = pl.multiple_of(i * chunk, chunk)
            block = ref[:, pl.ds(at, chunk)].astype(jnp.float32).T
            out[pl.ds(k * lat + at, chunk), :] = block.astype(out.dtype)


def turn(*codes):
    tokens, lat = codes[0].shape
    return pl.pallas_call(
        functools.partial(turn_kernel, min(512, lat)),
        out_shape=jax.ShapeDtypeStruct((len(codes) * lat, tokens), codes[0].dtype),
        in_specs=[WHOLE] * len(codes),
        out_specs=WHOLE,
        cost_estimate=waits(4),
        compiler_params=params(8),
    )(*codes)


def sum_kernel(own, far, out, sent):
    me = lax.axis_index("latent") // 2
    total = own[...]
    for j in range(1, far.shape[0]):
        total = total + far[me ^ j]
    out[...] = total
    sent[...] = total.astype(sent.dtype)


def add_up(own, far):
    return pl.pallas_call(
        sum_kernel,
        out_shape=[
            jax.ShapeDtypeStruct(own.shape, jnp.float32),
            jax.ShapeDtypeStruct(own.shape, jnp.bfloat16),
        ],
        in_specs=[WHOLE] * 2,
        out_specs=[WHOLE] * 2,
        cost_estimate=waits(8),
        compiler_params=params(4),
    )(own, far)


def error_kernel(total, rows, *refs):
    *near, out = refs
    total = total[...]
    for ref in near:
        half = ref.shape[0] // 2
        term = ref[...].astype(jnp.float32)
        total = total + jnp.concatenate([term[half:], term[:half]])
    err = (total - rows[...].astype(jnp.float32)).astype(out.dtype)
    for j in range(out.shape[0]):
        out[j] = err


def error(total, near, rows, copies):
    return pl.pallas_call(
        error_kernel,
        out_shape=jax.ShapeDtypeStruct((copies, *rows.shape), rows.dtype),
        in_specs=[WHOLE] * (2 + len(near)),
        out_specs=WHOLE,
        cost_estimate=waits(8),
        compiler_params=params(4),
    )(total, rows, *near)


def far_exchange(blocks):
    n = lax.axis_size("latent")
    groups = [list(range(near, n, 2)) for near in range(2)]
    return lax.all_to_all(blocks, "latent", 0, 0, axis_index_groups=groups, tiled=True)


def all_errors(sums, rows, codes_t):
    if lax.axis_size("latent") > DIRECT:
        total = lax.psum_scatter(sums[0], "latent", scatter_dimension=0, tiled=True)
        err = error(total, [], rows, 1)[0]
        return lax.all_gather(err, "latent", axis=0, tiled=True)[None], codes_t
    total, sent = add_up(sums[0], far_exchange(sums[1]))
    err = error(total, [swap(sent, "latent", 1)], rows, sums[1].shape[0])
    err, codes_t = lax.optimization_barrier((err, codes_t))
    return far_exchange(err), codes_t


def adam_kernel(codes_t, m, v, blocks, out, product, err):
    tokens = codes_t.shape[1]
    b = 0.1 / (1.0 - 0.9**10) / tokens
    a = 0.9 / (1.0 - 0.9**10) / b
    p = 0.999 / (1.0 - 0.999**10) / b**2
    q = 0.001 / (1.0 - 0.999**10) / tokens**2 / b**2
    eps = 1e-8 / b
    i, last = pl.program_id(0), pl.num_programs(0) - 1
    rows = out.shape[0]
    part = product.shape[0]
    slab = 16

    def multiply(start):
        at = pl.ds(pl.multiple_of(start, part), part)
        return jnp.dot(codes_t[at, :], err[...], preferred_element_type=jnp.float32)

    @pl.when(i == 0)
    def _():
        me = lax.axis_index("latent") // 2
        n = blocks.shape[0]
        picked = [blocks[me ^ j if n > 1 else 0] for j in range(n)]
        err[...] = jnp.concatenate([x.astype(jnp.float32) for x in picked]).astype(err.dtype)
        product[...] = multiply(0)

    def direction(c, start):
        at = pl.ds(pl.multiple_of(start, slab), slab)
        first = m[at, :].astype(jnp.float32) * a + c
        second = v[at, :].astype(jnp.float32) * p + (c * c) * q
        root = second * lax.rsqrt(second)
        return (first * pl.reciprocal(root + eps, approx=True)).astype(out.dtype)

    c = product[...]
    done = []
    for k in range(0, rows, part):
        if k + part < rows:
            later = multiply(i * rows + k + part)
        else:
            later = multiply(jnp.minimum(i + 1, last) * rows)
        steps = [(k + r, direction(c[r : r + slab], i * rows + k + r)) for r in range(0, part, slab)]
        for r, step in done:
            out[r : r + slab, :] = step
        done, c = steps, later
    for r, step in done:
        out[r : r + slab, :] = step
    product[...] = c


def adam(codes_t, blocks, m, v):
    lat, half = m.shape
    rows = min(1024, lat)
    return pl.pallas_call(
        adam_kernel,
        grid=(lat // rows,),
        out_shape=jax.ShapeDtypeStruct(m.shape, jnp.bfloat16),
        in_specs=[WHOLE] * 4,
        out_specs=pl.BlockSpec((rows, half), lambda i: (i, 0)),
        scratch_shapes=[
            pltpu.VMEM((64, half), jnp.float32),
            pltpu.VMEM((codes_t.shape[1], half), jnp.bfloat16),
        ],
        compiler_params=params(12),
    )(codes_t, resident(m), resident(v), blocks)


def per_device(acts, w_enc, b_enc, w_dec, dec_m, dec_v):
    direct = lax.axis_size("latent") <= DIRECT
    rows = near_rows(acts, 2 if direct else 1)
    blocks = spread(rows)
    part = w_enc.shape[1] // 2
    mine = [encode(blocks, w_enc, k * part, part) for k in range(2)]
    theirs = [swap(x, "dp", 1) for x in mine]
    codes, sums = [None, None], []
    for k in range(2):
        codes[k], sums = decode(
            mine[k], theirs[k], b_enc, w_dec, k * part, sums, len(blocks) if k else 1
        )
    errors, codes_t = all_errors(sums, rows, turn(*codes))
    return adam(codes_t, errors, dec_m, dec_v)


def solution(mesh):
    in_specs = (
        P(("groups", "latent", "dp"), None),
        P(("groups", "dp"), "latent"),
        P(("groups", "latent")),
        P(("groups", "latent"), "dp"),
        P(("groups", "latent"), "dp"),
        P(("groups", "latent"), "dp"),
    )
    out_specs = P(("groups", "latent"), "dp")
    return jax.shard_map(
        per_device, mesh=mesh, in_specs=in_specs, out_specs=out_specs, check_vma=False
    )
```

```python
import functools

import jax
import jax.numpy as jnp
from jax import lax
from jax.experimental import pallas as pl
from jax.experimental.pallas import tpu as pltpu
from jax.sharding import PartitionSpec as P

MIB = 1 << 20
WHOLE = pl.BlockSpec(memory_space=pltpu.VMEM)
DIRECT = 8


def swap(value, axis, mask):
    n = lax.axis_size(axis)
    return lax.ppermute(value, axis, [(i, i ^ mask) for i in range(n)])


def params(mib):
    return pltpu.CompilerParams(vmem_limit_bytes=mib * MIB)


def waits(mib):
    return pl.CostEstimate(flops=mib * 350_000_000, bytes_accessed=mib * MIB, transcendentals=0)


def resident(value):
    return pltpu.with_memory_space_constraint(value, pltpu.VMEM)


def far_masks():
    return range(2, lax.axis_size("latent"), 2)


def stack(refs):
    return jnp.concatenate([r[...].astype(jnp.float32) for r in refs]).astype(refs[0].dtype)


def near_kernel(*refs):
    *rows, out = refs
    half = out.shape[1]
    side = lax.axis_index("dp")

    def write(order, at):
        picked = [rows[i][:, at : at + half].astype(jnp.float32) for i in order]
        out[...] = jnp.concatenate(picked).astype(out.dtype)

    pairs = range(0, len(rows), 2)

    @pl.when(side == 0)
    def _():
        write([i + c for i in pairs for c in (0, 1)], 0)

    @pl.when(side == 1)
    def _():
        write([i + c for i in pairs for c in (1, 0)], half)


def copy_kernel(x, out):
    out[...] = x[...]


def near_rows(acts, near):
    axes = ("latent", "dp")
    own = pl.pallas_call(
        copy_kernel,
        out_shape=jax.ShapeDtypeStruct(acts.shape, acts.dtype),
        in_specs=[WHOLE],
        out_specs=WHOLE,
        cost_estimate=waits(1),
        compiler_params=params(4),
    )(acts)
    rows = [own] + [swap(acts, axes, mask) for mask in range(1, 2 * near)]
    return pl.pallas_call(
        near_kernel,
        out_shape=jax.ShapeDtypeStruct((len(rows) * acts.shape[0], acts.shape[1] // 2), acts.dtype),
        in_specs=[WHOLE] * len(rows),
        out_specs=WHOLE,
        cost_estimate=waits(14),
        compiler_params=params(4),
    )(*rows)


def spread(block):
    if lax.axis_size("latent") > DIRECT:
        return [lax.all_gather(block, "latent", axis=0, tiled=True)]
    return [block] + [swap(block, "latent", mask) for mask in far_masks()]


def encode_kernel(first, *refs):
    *rows_refs, w, out = refs
    lat = out.shape[1]
    out[...] = jnp.dot(
        stack(rows_refs), w[:, first : first + lat], preferred_element_type=jnp.float32
    )


def encode(blocks, w_enc, first, lat):
    tokens = sum(b.shape[0] for b in blocks)
    return pl.pallas_call(
        functools.partial(encode_kernel, first),
        out_shape=jax.ShapeDtypeStruct((tokens, lat), jnp.float32),
        in_specs=[WHOLE] * (len(blocks) + 1),
        out_specs=WHOLE,
        cost_estimate=waits(7),
        compiler_params=params(8),
    )(*blocks, resident(w_enc))


def decode_kernel(first, given, mine, theirs, bias, w, *refs):
    codes, *out = refs[given:]
    lat = mine.shape[1]
    pre = mine[...] + theirs[...] + bias[:, first : first + lat]
    block = jnp.maximum(pre, 0.0).astype(jnp.bfloat16)
    codes[...] = block
    total = jnp.dot(block, w[first : first + lat, :], preferred_element_type=jnp.float32)
    if given:
        total = total + refs[0][...]
    rows = out[0].shape[0]
    for j, ref in enumerate(out):
        ref[...] = total[j * rows : (j + 1) * rows].astype(ref.dtype)


def decode(mine, theirs, bias, w_dec, first, given, far):
    tokens, lat = mine.shape
    half = w_dec.shape[1]
    sums = [
        jax.ShapeDtypeStruct((tokens // far, half), jnp.bfloat16 if j else jnp.float32)
        for j in range(far)
    ]
    codes, *sums = pl.pallas_call(
        functools.partial(decode_kernel, first, len(given)),
        out_shape=[jax.ShapeDtypeStruct((tokens, lat), jnp.bfloat16)] + sums,
        in_specs=[WHOLE] * (4 + len(given)),
        out_specs=[WHOLE] * (1 + len(sums)),
        cost_estimate=waits(7),
        compiler_params=params(8),
    )(mine, theirs, bias.reshape(1, -1), resident(w_dec), *given)
    return codes, sums


def turn_kernel(chunk, *refs):
    *codes, out = refs
    for k, ref in enumerate(codes):
        lat = ref.shape[1]

        @pl.loop(0, lat // chunk)
        def _(i):
            at = pl.multiple_of(i * chunk, chunk)
            block = ref[:, pl.ds(at, chunk)].astype(jnp.float32).T
            out[pl.ds(k * lat + at, chunk), :] = block.astype(out.dtype)


def turn(*codes):
    tokens, lat = codes[0].shape
    return pl.pallas_call(
        functools.partial(turn_kernel, min(512, lat)),
        out_shape=jax.ShapeDtypeStruct((len(codes) * lat, tokens), codes[0].dtype),
        in_specs=[WHOLE] * len(codes),
        out_specs=WHOLE,
        cost_estimate=waits(4),
        compiler_params=params(8),
    )(*codes)


def sum_kernel(own, *refs):
    *terms, out, sent = refs
    total = own[...]
    for ref in terms:
        total = total + ref[...]
    out[...] = total
    sent[...] = total.astype(sent.dtype)


def add_up(terms):
    shape = terms[0].shape
    return pl.pallas_call(
        sum_kernel,
        out_shape=[
            jax.ShapeDtypeStruct(shape, jnp.float32),
            jax.ShapeDtypeStruct(shape, jnp.bfloat16),
        ],
        in_specs=[WHOLE] * len(terms),
        out_specs=[WHOLE] * 2,
        cost_estimate=waits(8),
        compiler_params=params(4),
    )(*terms)


def error_kernel(total, rows, *refs):
    *near, out = refs
    total = total[...]
    for ref in near:
        half = ref.shape[0] // 2
        term = ref[...].astype(jnp.float32)
        total = total + jnp.concatenate([term[half:], term[:half]])
    out[...] = (total - rows[...].astype(jnp.float32)).astype(out.dtype)


def error(total, near, rows):
    return pl.pallas_call(
        error_kernel,
        out_shape=jax.ShapeDtypeStruct(rows.shape, rows.dtype),
        in_specs=[WHOLE] * (2 + len(near)),
        out_specs=WHOLE,
        cost_estimate=waits(8),
        compiler_params=params(4),
    )(total, rows, *near)


def reduce_rows(sums):
    if lax.axis_size("latent") > DIRECT:
        return lax.psum_scatter(sums[0], "latent", scatter_dimension=0, tiled=True), []
    terms = [sums[0]] + [swap(s, "latent", mask) for s, mask in zip(sums[1:], far_masks())]
    total, sent = add_up(terms)
    return total, [swap(sent, "latent", 1)]


def adam_kernel(codes_t, m, v, *refs):
    *blocks, out, product, err = refs
    tokens = codes_t.shape[1]
    b = 0.1 / (1.0 - 0.9**10) / tokens
    a = 0.9 / (1.0 - 0.9**10) / b
    p = 0.999 / (1.0 - 0.999**10) / b**2
    q = 0.001 / (1.0 - 0.999**10) / tokens**2 / b**2
    eps = 1e-8 / b
    i, last = pl.program_id(0), pl.num_programs(0) - 1
    rows = out.shape[0]
    part = product.shape[0]
    slab = 16

    def multiply(start):
        at = pl.ds(pl.multiple_of(start, part), part)
        return jnp.dot(codes_t[at, :], err[...], preferred_element_type=jnp.float32)

    @pl.when(i == 0)
    def _():
        err[...] = stack(blocks)
        product[...] = multiply(0)

    def direction(c, start):
        at = pl.ds(pl.multiple_of(start, slab), slab)
        first = m[at, :].astype(jnp.float32) * a + c
        second = v[at, :].astype(jnp.float32) * p + (c * c) * q
        inverse = lax.rsqrt(second)
        x = inverse * eps
        return (first * (inverse * (1.0 - x * (1.0 - x)))).astype(out.dtype)

    c = product[...]
    done = []
    for k in range(0, rows, part):
        if k + part < rows:
            later = multiply(i * rows + k + part)
        else:
            later = multiply(jnp.minimum(i + 1, last) * rows)
        steps = [(k + r, direction(c[r : r + slab], i * rows + k + r)) for r in range(0, part, slab)]
        for r, step in done:
            out[r : r + slab, :] = step
        done, c = steps, later
    for r, step in done:
        out[r : r + slab, :] = step
    product[...] = c


def adam(codes_t, blocks, m, v):
    lat, half = m.shape
    rows = min(1024, lat)
    return pl.pallas_call(
        adam_kernel,
        grid=(lat // rows,),
        out_shape=jax.ShapeDtypeStruct(m.shape, jnp.bfloat16),
        in_specs=[WHOLE] * (3 + len(blocks)),
        out_specs=pl.BlockSpec((rows, half), lambda i: (i, 0)),
        scratch_shapes=[
            pltpu.VMEM((64, half), jnp.float32),
            pltpu.VMEM((codes_t.shape[1], half), jnp.bfloat16),
        ],
        compiler_params=params(12),
    )(codes_t, resident(m), resident(v), *blocks)


def per_device(acts, w_enc, b_enc, w_dec, dec_m, dec_v):
    direct = lax.axis_size("latent") <= DIRECT
    rows = near_rows(acts, 2 if direct else 1)
    blocks = spread(rows)
    part = w_enc.shape[1] // 2
    mine = [encode(blocks, w_enc, k * part, part) for k in range(2)]
    theirs = [swap(x, "dp", 1) for x in mine]
    codes, sums = [None, None], []
    for k in range(2):
        codes[k], sums = decode(
            mine[k], theirs[k], b_enc, w_dec, k * part, sums, len(blocks) if k else 1
        )
    codes_t = turn(*codes)
    total, near = reduce_rows(sums)
    err = spread(error(total, near, rows))
    return adam(codes_t, err, dec_m, dec_v)


def solution(mesh):
    in_specs = (
        P(("groups", "latent", "dp"), None),
        P(("groups", "dp"), "latent"),
        P(("groups", "latent")),
        P(("groups", "latent"), "dp"),
        P(("groups", "latent"), "dp"),
        P(("groups", "latent"), "dp"),
    )
    out_specs = P(("groups", "latent"), "dp")
    return jax.shard_map(
        per_device, mesh=mesh, in_specs=in_specs, out_specs=out_specs, check_vma=False
    )
```

```python
import functools

import jax
import jax.numpy as jnp
from jax import lax
from jax.experimental import pallas as pl
from jax.experimental.pallas import tpu as pltpu
from jax.sharding import PartitionSpec as P

MIB = 1 << 20
WHOLE = pl.BlockSpec(memory_space=pltpu.VMEM)
DIRECT = 8


def swap(value, axis, mask):
    n = lax.axis_size(axis)
    return lax.ppermute(value, axis, [(i, i ^ mask) for i in range(n)])


def params(mib):
    return pltpu.CompilerParams(vmem_limit_bytes=mib * MIB)


def waits(mib):
    return pl.CostEstimate(flops=mib * 350_000_000, bytes_accessed=mib * MIB, transcendentals=0)


def resident(value):
    return pltpu.with_memory_space_constraint(value, pltpu.VMEM)


def far_masks():
    return range(2, lax.axis_size("latent"), 2)


def stack(refs):
    return jnp.concatenate([r[...].astype(jnp.float32) for r in refs]).astype(refs[0].dtype)


def near_kernel(*refs):
    *rows, out = refs
    half = out.shape[1]
    side = lax.axis_index("dp")

    def write(order, at):
        picked = [rows[i][:, at : at + half].astype(jnp.float32) for i in order]
        out[...] = jnp.concatenate(picked).astype(out.dtype)

    pairs = range(0, len(rows), 2)

    @pl.when(side == 0)
    def _():
        write([i + c for i in pairs for c in (0, 1)], 0)

    @pl.when(side == 1)
    def _():
        write([i + c for i in pairs for c in (1, 0)], half)


def copy_kernel(x, out):
    out[...] = x[...]


def near_rows(acts, near):
    axes = ("latent", "dp")
    own = pl.pallas_call(
        copy_kernel,
        out_shape=jax.ShapeDtypeStruct(acts.shape, acts.dtype),
        in_specs=[WHOLE],
        out_specs=WHOLE,
        cost_estimate=waits(1),
        compiler_params=params(4),
    )(acts)
    rows = [own] + [swap(acts, axes, mask) for mask in range(1, 2 * near)]
    return pl.pallas_call(
        near_kernel,
        out_shape=jax.ShapeDtypeStruct((len(rows) * acts.shape[0], acts.shape[1] // 2), acts.dtype),
        in_specs=[WHOLE] * len(rows),
        out_specs=WHOLE,
        cost_estimate=waits(14),
        compiler_params=params(4),
    )(*rows)


def spread(block):
    if lax.axis_size("latent") > DIRECT:
        return [lax.all_gather(block, "latent", axis=0, tiled=True)]
    return [block] + [swap(block, "latent", mask) for mask in far_masks()]


def encode_kernel(first, *refs):
    *rows_refs, w, out = refs
    lat = out.shape[1]
    out[...] = jnp.dot(
        stack(rows_refs), w[:, first : first + lat], preferred_element_type=jnp.float32
    )


def encode(blocks, w_enc, first, lat):
    tokens = sum(b.shape[0] for b in blocks)
    return pl.pallas_call(
        functools.partial(encode_kernel, first),
        out_shape=jax.ShapeDtypeStruct((tokens, lat), jnp.float32),
        in_specs=[WHOLE] * (len(blocks) + 1),
        out_specs=WHOLE,
        cost_estimate=waits(7),
        compiler_params=params(8),
    )(*blocks, resident(w_enc))


def decode_kernel(first, given, mine, theirs, bias, w, *refs):
    codes, *out = refs[given:]
    lat = mine.shape[1]
    pre = mine[...] + theirs[...] + bias[:, first : first + lat]
    block = jnp.maximum(pre, 0.0).astype(jnp.bfloat16)
    codes[...] = block
    total = jnp.dot(block, w[first : first + lat, :], preferred_element_type=jnp.float32)
    if given:
        total = total + refs[0][...]
    rows = out[0].shape[0]
    for j, ref in enumerate(out):
        ref[...] = total[j * rows : (j + 1) * rows].astype(ref.dtype)


def decode(mine, theirs, bias, w_dec, first, given, far):
    tokens, lat = mine.shape
    half = w_dec.shape[1]
    sums = [
        jax.ShapeDtypeStruct((tokens // far, half), jnp.bfloat16 if j else jnp.float32)
        for j in range(far)
    ]
    codes, *sums = pl.pallas_call(
        functools.partial(decode_kernel, first, len(given)),
        out_shape=[jax.ShapeDtypeStruct((tokens, lat), jnp.bfloat16)] + sums,
        in_specs=[WHOLE] * (4 + len(given)),
        out_specs=[WHOLE] * (1 + len(sums)),
        cost_estimate=waits(7),
        compiler_params=params(8),
    )(mine, theirs, bias.reshape(1, -1), resident(w_dec), *given)
    return codes, sums


def turn_kernel(chunk, *refs):
    *codes, out = refs
    for k, ref in enumerate(codes):
        lat = ref.shape[1]

        @pl.loop(0, lat // chunk)
        def _(i):
            at = pl.multiple_of(i * chunk, chunk)
            block = ref[:, pl.ds(at, chunk)].astype(jnp.float32).T
            out[pl.ds(k * lat + at, chunk), :] = block.astype(out.dtype)


def turn(*codes):
    tokens, lat = codes[0].shape
    return pl.pallas_call(
        functools.partial(turn_kernel, min(512, lat)),
        out_shape=jax.ShapeDtypeStruct((len(codes) * lat, tokens), codes[0].dtype),
        in_specs=[WHOLE] * len(codes),
        out_specs=WHOLE,
        cost_estimate=waits(4),
        compiler_params=params(8),
    )(*codes)


def sum_kernel(own, *refs):
    *terms, out = refs
    total = own[...]
    for ref in terms:
        total = total + ref[...]
    out[...] = total


def add_up(terms):
    return pl.pallas_call(
        sum_kernel,
        out_shape=jax.ShapeDtypeStruct(terms[0].shape, jnp.float32),
        in_specs=[WHOLE] * len(terms),
        out_specs=WHOLE,
        cost_estimate=waits(8),
        compiler_params=params(4),
    )(*terms)


def error_kernel(total, rows, *refs):
    *near, out = refs
    total = total[...]
    for ref in near:
        half = ref.shape[0] // 2
        total = total + jnp.concatenate([ref[half:], ref[:half]])
    out[...] = (total - rows[...].astype(jnp.float32)).astype(out.dtype)


def error(total, near, rows):
    return pl.pallas_call(
        error_kernel,
        out_shape=jax.ShapeDtypeStruct(rows.shape, rows.dtype),
        in_specs=[WHOLE] * (2 + len(near)),
        out_specs=WHOLE,
        cost_estimate=waits(8),
        compiler_params=params(4),
    )(total, rows, *near)


def reduce_rows(sums):
    if lax.axis_size("latent") > DIRECT:
        return lax.psum_scatter(sums[0], "latent", scatter_dimension=0, tiled=True), []
    terms = [sums[0]] + [swap(s, "latent", mask) for s, mask in zip(sums[1:], far_masks())]
    total = add_up(terms)
    return total, [swap(total, "latent", 1)]


def adam_kernel(codes_t, m, v, *refs):
    *blocks, out, product, err = refs
    tokens = codes_t.shape[1]
    b = 0.1 / (1.0 - 0.9**10) / tokens
    a = 0.9 / (1.0 - 0.9**10) / b
    p = 0.999 / (1.0 - 0.999**10) / b**2
    q = 0.001 / (1.0 - 0.999**10) / tokens**2 / b**2
    eps = 1e-8 / b
    i, last = pl.program_id(0), pl.num_programs(0) - 1
    rows = out.shape[0]
    part = product.shape[0]
    slab = 16

    def multiply(start):
        at = pl.ds(pl.multiple_of(start, part), part)
        return jnp.dot(codes_t[at, :], err[...], preferred_element_type=jnp.float32)

    @pl.when(i == 0)
    def _():
        err[...] = stack(blocks)
        product[...] = multiply(0)

    a, p, q, eps = (jnp.asarray(x, out.dtype) for x in (a, p, q, eps))

    def direction(c, start):
        at = pl.ds(pl.multiple_of(start, slab), slab)
        c = c.astype(out.dtype)
        first = m[at, :] * a + c
        second = v[at, :] * p + (c * c) * q
        root = second * lax.rsqrt(second)
        return first * pl.reciprocal(root + eps, approx=True)

    c = product[...]
    done = []
    for k in range(0, rows, part):
        if k + part < rows:
            later = multiply(i * rows + k + part)
        else:
            later = multiply(jnp.minimum(i + 1, last) * rows)
        steps = [(k + r, direction(c[r : r + slab], i * rows + k + r)) for r in range(0, part, slab)]
        for r, step in done:
            out[r : r + slab, :] = step
        done, c = steps, later
    for r, step in done:
        out[r : r + slab, :] = step
    product[...] = c


def adam(codes_t, blocks, m, v):
    lat, half = m.shape
    rows = min(1024, lat)
    return pl.pallas_call(
        adam_kernel,
        grid=(lat // rows,),
        out_shape=jax.ShapeDtypeStruct(m.shape, jnp.bfloat16),
        in_specs=[WHOLE] * (3 + len(blocks)),
        out_specs=pl.BlockSpec((rows, half), lambda i: (i, 0)),
        scratch_shapes=[
            pltpu.VMEM((64, half), jnp.float32),
            pltpu.VMEM((codes_t.shape[1], half), jnp.bfloat16),
        ],
        compiler_params=params(12),
    )(codes_t, resident(m), resident(v), *blocks)


def per_device(acts, w_enc, b_enc, w_dec, dec_m, dec_v):
    direct = lax.axis_size("latent") <= DIRECT
    rows = near_rows(acts, 2 if direct else 1)
    blocks = spread(rows)
    part = w_enc.shape[1] // 2
    mine = [encode(blocks, w_enc, k * part, part) for k in range(2)]
    theirs = [swap(x, "dp", 1) for x in mine]
    codes, sums = [None, None], []
    for k in range(2):
        codes[k], sums = decode(
            mine[k], theirs[k], b_enc, w_dec, k * part, sums, len(blocks) if k else 1
        )
    codes_t = turn(*codes)
    total, near = reduce_rows(sums)
    err = spread(error(total, near, rows))
    return adam(codes_t, err, dec_m, dec_v)


def solution(mesh):
    in_specs = (
        P(("groups", "latent", "dp"), None),
        P(("groups", "dp"), "latent"),
        P(("groups", "latent")),
        P(("groups", "latent"), "dp"),
        P(("groups", "latent"), "dp"),
        P(("groups", "latent"), "dp"),
    )
    out_specs = P(("groups", "latent"), "dp")
    return jax.shard_map(
        per_device, mesh=mesh, in_specs=in_specs, out_specs=out_specs, check_vma=False
    )
```

```python
import functools

import jax
import jax.numpy as jnp
from jax import lax
from jax.experimental import pallas as pl
from jax.experimental.pallas import tpu as pltpu
from jax.sharding import PartitionSpec as P

MIB = 1 << 20
PARTS = 2
WHOLE = pl.BlockSpec(memory_space=pltpu.VMEM)
DIRECT = 8


def swap(value, axis, mask):
    n = lax.axis_size(axis)
    return lax.ppermute(value, axis, [(i, i ^ mask) for i in range(n)])


def params(mib):
    return pltpu.CompilerParams(vmem_limit_bytes=mib * MIB)


def waits(mib):
    return pl.CostEstimate(flops=mib * 350_000_000, bytes_accessed=mib * MIB, transcendentals=0)


def resident(value):
    return pltpu.with_memory_space_constraint(value, pltpu.VMEM)


def far_masks():
    return range(2, lax.axis_size("latent"), 2)


def stack(refs):
    return jnp.concatenate([r[...].astype(jnp.float32) for r in refs]).astype(refs[0].dtype)


def near_kernel(*refs):
    *rows, out = refs
    half = out.shape[1]
    side = lax.axis_index("dp")

    def write(order, at):
        picked = [rows[i][:, at : at + half].astype(jnp.float32) for i in order]
        out[...] = jnp.concatenate(picked).astype(out.dtype)

    pairs = range(0, len(rows), 2)

    @pl.when(side == 0)
    def _():
        write([i + c for i in pairs for c in (0, 1)], 0)

    @pl.when(side == 1)
    def _():
        write([i + c for i in pairs for c in (1, 0)], half)


def copy_kernel(x, out):
    out[...] = x[...]


def near_rows(acts, near):
    axes = ("latent", "dp")
    own = pl.pallas_call(
        copy_kernel,
        out_shape=jax.ShapeDtypeStruct(acts.shape, acts.dtype),
        in_specs=[WHOLE],
        out_specs=WHOLE,
        cost_estimate=waits(1),
        compiler_params=params(4),
    )(acts)
    rows = [own] + [swap(acts, axes, mask) for mask in range(1, 2 * near)]
    return pl.pallas_call(
        near_kernel,
        out_shape=jax.ShapeDtypeStruct((len(rows) * acts.shape[0], acts.shape[1] // 2), acts.dtype),
        in_specs=[WHOLE] * len(rows),
        out_specs=WHOLE,
        cost_estimate=waits(14),
        compiler_params=params(4),
    )(*rows)


def spread(block):
    if lax.axis_size("latent") > DIRECT:
        return [lax.all_gather(block, "latent", axis=0, tiled=True)]
    return [block] + [swap(block, "latent", mask) for mask in far_masks()]


def encode_kernel(first, *refs):
    *rows_refs, w, out = refs
    lat = out.shape[1]
    out[...] = jnp.dot(
        stack(rows_refs), w[:, first : first + lat], preferred_element_type=jnp.float32
    )


def encode(blocks, w_enc, first, lat):
    tokens = sum(b.shape[0] for b in blocks)
    return pl.pallas_call(
        functools.partial(encode_kernel, first),
        out_shape=jax.ShapeDtypeStruct((tokens, lat), jnp.float32),
        in_specs=[WHOLE] * (len(blocks) + 1),
        out_specs=WHOLE,
        cost_estimate=waits(7),
        compiler_params=params(8),
    )(*blocks, resident(w_enc))


def decode_kernel(first, given, mine, theirs, bias, w, *refs):
    codes, *out = refs[given:]
    lat = mine.shape[1]
    pre = mine[...] + theirs[...] + bias[:, first : first + lat]
    block = jnp.maximum(pre, 0.0).astype(jnp.bfloat16)
    codes[...] = block
    total = jnp.dot(block, w[first : first + lat, :], preferred_element_type=jnp.float32)
    if given:
        total = total + refs[0][...]
    rows = out[0].shape[0]
    for j, ref in enumerate(out):
        ref[...] = total[j * rows : (j + 1) * rows].astype(ref.dtype)


def decode(mine, theirs, bias, w_dec, first, given, far):
    tokens, lat = mine.shape
    half = w_dec.shape[1]
    sums = [
        jax.ShapeDtypeStruct((tokens // far, half), jnp.bfloat16 if j else jnp.float32)
        for j in range(far)
    ]
    codes, *sums = pl.pallas_call(
        functools.partial(decode_kernel, first, len(given)),
        out_shape=[jax.ShapeDtypeStruct((tokens, lat), jnp.bfloat16)] + sums,
        in_specs=[WHOLE] * (4 + len(given)),
        out_specs=[WHOLE] * (1 + len(sums)),
        cost_estimate=waits(7),
        compiler_params=params(8),
    )(mine, theirs, bias.reshape(1, -1), resident(w_dec), *given)
    return codes, sums


def turn_kernel(chunk, *refs):
    *codes, out = refs
    for k, ref in enumerate(codes):
        lat = ref.shape[1]

        @pl.loop(0, lat // chunk)
        def _(i):
            at = pl.multiple_of(i * chunk, chunk)
            block = ref[:, pl.ds(at, chunk)].astype(jnp.float32).T
            out[pl.ds(k * lat + at, chunk), :] = block.astype(out.dtype)


def turn(*codes):
    tokens, lat = codes[0].shape
    return pl.pallas_call(
        functools.partial(turn_kernel, min(512, lat)),
        out_shape=jax.ShapeDtypeStruct((len(codes) * lat, tokens), codes[0].dtype),
        in_specs=[WHOLE] * len(codes),
        out_specs=WHOLE,
        cost_estimate=waits(4),
        compiler_params=params(8),
    )(*codes)


def sum_kernel(own, *refs):
    *terms, out = refs
    total = own[...]
    for ref in terms:
        total = total + ref[...]
    out[...] = total


def add_up(terms):
    return pl.pallas_call(
        sum_kernel,
        out_shape=jax.ShapeDtypeStruct(terms[0].shape, jnp.float32),
        in_specs=[WHOLE] * len(terms),
        out_specs=WHOLE,
        cost_estimate=waits(8),
        compiler_params=params(4),
    )(*terms)


def error_kernel(total, rows, *refs):
    *near, out = refs
    total = total[...]
    for ref in near:
        half = ref.shape[0] // 2
        total = total + jnp.concatenate([ref[half:], ref[:half]])
    out[...] = (total - rows[...].astype(jnp.float32)).astype(out.dtype)


def error(total, near, rows):
    return pl.pallas_call(
        error_kernel,
        out_shape=jax.ShapeDtypeStruct(rows.shape, rows.dtype),
        in_specs=[WHOLE] * (2 + len(near)),
        out_specs=WHOLE,
        cost_estimate=waits(8),
        compiler_params=params(4),
    )(total, rows, *near)


def reduce_rows(sums):
    if lax.axis_size("latent") > DIRECT:
        return lax.psum_scatter(sums[0], "latent", scatter_dimension=0, tiled=True), []
    terms = [sums[0]] + [swap(s, "latent", mask) for s, mask in zip(sums[1:], far_masks())]
    total = add_up(terms)
    return total, [swap(total, "latent", 1)]


def adam_kernel(codes_t, m, v, *refs):
    *blocks, out, even, odd, err = refs
    products = (even, odd)
    tokens = codes_t.shape[1]
    b = 0.1 / (1.0 - 0.9**10) / tokens
    a = 0.9 / (1.0 - 0.9**10) / b
    p = 0.999 / (1.0 - 0.999**10) / b**2
    q = 0.001 / (1.0 - 0.999**10) / tokens**2 / b**2
    a, p, q, eps = (jnp.asarray(x, out.dtype) for x in (a, p, q, 1e-8 / b))
    i, last = pl.program_id(0), pl.num_programs(0) - 1
    rows = out.shape[0]
    part = even.shape[0]
    slab = 16

    def multiply(start, product):
        at = pl.ds(pl.multiple_of(start, part), part)
        c = jnp.dot(codes_t[at, :], err[...], preferred_element_type=jnp.float32)
        product[...] = c.astype(product.dtype)

    @pl.when(i == 0)
    def _():
        err[...] = stack(blocks)
        multiply(0, even)

    for k in range(2):
        if k == 0:
            multiply(i * rows + part, odd)
        else:
            multiply(jnp.minimum(i + 1, last) * rows, even)
        for r in range(0, part, slab):
            at = pl.ds(pl.multiple_of(i * rows + k * part + r, slab), slab)
            c = products[k][r : r + slab, :]
            first = m[at, :] * a + c
            second = v[at, :] * p + (c * c) * q
            root = second * lax.rsqrt(second)
            step = first * pl.reciprocal(root + eps, approx=True)
            out[k * part + r : k * part + r + slab, :] = step


def adam(codes_t, blocks, m, v):
    lat, half = m.shape
    rows = min(1024, lat)
    return pl.pallas_call(
        adam_kernel,
        grid=(lat // rows,),
        out_shape=jax.ShapeDtypeStruct(m.shape, jnp.bfloat16),
        in_specs=[WHOLE] * (3 + len(blocks)),
        out_specs=pl.BlockSpec((rows, half), lambda i: (i, 0)),
        scratch_shapes=[pltpu.VMEM((rows // 2, half), jnp.bfloat16)] * 2
        + [pltpu.VMEM((codes_t.shape[1], half), jnp.bfloat16)],
        compiler_params=params(12),
    )(codes_t, resident(m), resident(v), *blocks)


def per_device(acts, w_enc, b_enc, w_dec, dec_m, dec_v):
    direct = lax.axis_size("latent") <= DIRECT
    rows = near_rows(acts, 2 if direct else 1)
    blocks = spread(rows)
    part = w_enc.shape[1] // PARTS
    mine = [encode(blocks, w_enc, k * part, part) for k in range(PARTS)]
    theirs = [swap(x, "dp", 1) for x in mine]
    codes, sums = [], []
    for k in range(PARTS):
        far = len(blocks) if k == PARTS - 1 else 1
        block, sums = decode(mine[k], theirs[k], b_enc, w_dec, k * part, sums, far)
        codes.append(block)
    codes_t = turn(*codes)
    total, near = reduce_rows(sums)
    err = spread(error(total, near, rows))
    return adam(codes_t, err, dec_m, dec_v)


def solution(mesh):
    in_specs = (
        P(("groups", "latent", "dp"), None),
        P(("groups", "dp"), "latent"),
        P(("groups", "latent")),
        P(("groups", "latent"), "dp"),
        P(("groups", "latent"), "dp"),
        P(("groups", "latent"), "dp"),
    )
    out_specs = P(("groups", "latent"), "dp")
    return jax.shard_map(
        per_device, mesh=mesh, in_specs=in_specs, out_specs=out_specs, check_vma=False
    )
```

```python
import functools

import jax
import jax.numpy as jnp
from jax import lax
from jax.experimental import pallas as pl
from jax.experimental.pallas import tpu as pltpu
from jax.sharding import PartitionSpec as P

MIB = 1 << 20
PARTS = 2
WHOLE = pl.BlockSpec(memory_space=pltpu.VMEM)
DIRECT = 8


def swap(value, axis, mask):
    n = lax.axis_size(axis)
    return lax.ppermute(value, axis, [(i, i ^ mask) for i in range(n)])


def params(mib):
    return pltpu.CompilerParams(vmem_limit_bytes=mib * MIB)


def waits(mib):
    return pl.CostEstimate(flops=mib * 350_000_000, bytes_accessed=mib * MIB, transcendentals=0)


def resident(value):
    return pltpu.with_memory_space_constraint(value, pltpu.VMEM)


def far_masks():
    return range(2, lax.axis_size("latent"), 2)


def stack(refs):
    return jnp.concatenate([r[...].astype(jnp.float32) for r in refs]).astype(refs[0].dtype)


def near_kernel(*refs):
    *rows, out = refs
    half = out.shape[1]
    side = lax.axis_index("dp")

    def write(order, at):
        picked = [rows[i][:, at : at + half].astype(jnp.float32) for i in order]
        out[...] = jnp.concatenate(picked).astype(out.dtype)

    pairs = range(0, len(rows), 2)

    @pl.when(side == 0)
    def _():
        write([i + c for i in pairs for c in (0, 1)], 0)

    @pl.when(side == 1)
    def _():
        write([i + c for i in pairs for c in (1, 0)], half)


def copy_kernel(x, out):
    out[...] = x[...]


def near_rows(acts, near):
    axes = ("latent", "dp")
    own = pl.pallas_call(
        copy_kernel,
        out_shape=jax.ShapeDtypeStruct(acts.shape, acts.dtype),
        in_specs=[WHOLE],
        out_specs=WHOLE,
        cost_estimate=waits(1),
        compiler_params=params(4),
    )(acts)
    rows = [own] + [swap(acts, axes, mask) for mask in range(1, 2 * near)]
    return pl.pallas_call(
        near_kernel,
        out_shape=jax.ShapeDtypeStruct((len(rows) * acts.shape[0], acts.shape[1] // 2), acts.dtype),
        in_specs=[WHOLE] * len(rows),
        out_specs=WHOLE,
        cost_estimate=waits(14),
        compiler_params=params(4),
    )(*rows)


def spread(block):
    if lax.axis_size("latent") > DIRECT:
        return [lax.all_gather(block, "latent", axis=0, tiled=True)]
    return [block] + [swap(block, "latent", mask) for mask in far_masks()]


def encode_kernel(first, *refs):
    *rows_refs, w, out = refs
    lat = out.shape[1]
    out[...] = jnp.dot(
        stack(rows_refs), w[:, first : first + lat], preferred_element_type=jnp.float32
    )


def encode(blocks, w_enc, first, lat):
    tokens = sum(b.shape[0] for b in blocks)
    return pl.pallas_call(
        functools.partial(encode_kernel, first),
        out_shape=jax.ShapeDtypeStruct((tokens, lat), jnp.float32),
        in_specs=[WHOLE] * (len(blocks) + 1),
        out_specs=WHOLE,
        cost_estimate=waits(7),
        compiler_params=params(8),
    )(*blocks, resident(w_enc))


def decode_kernel(first, given, mine, theirs, bias, w, *refs):
    codes, *out = refs[given:]
    lat = mine.shape[1]
    pre = mine[...] + theirs[...] + bias[:, first : first + lat]
    block = jnp.maximum(pre, 0.0).astype(jnp.bfloat16)
    codes[...] = block
    total = jnp.dot(block, w[first : first + lat, :], preferred_element_type=jnp.float32)
    if given:
        total = total + refs[0][...]
    rows = out[0].shape[0]
    for j, ref in enumerate(out):
        ref[...] = total[j * rows : (j + 1) * rows].astype(ref.dtype)


def decode(mine, theirs, bias, w_dec, first, given, far):
    tokens, lat = mine.shape
    half = w_dec.shape[1]
    sums = [
        jax.ShapeDtypeStruct((tokens // far, half), jnp.bfloat16 if j else jnp.float32)
        for j in range(far)
    ]
    codes, *sums = pl.pallas_call(
        functools.partial(decode_kernel, first, len(given)),
        out_shape=[jax.ShapeDtypeStruct((tokens, lat), jnp.bfloat16)] + sums,
        in_specs=[WHOLE] * (4 + len(given)),
        out_specs=[WHOLE] * (1 + len(sums)),
        cost_estimate=waits(7),
        compiler_params=params(8),
    )(mine, theirs, bias.reshape(1, -1), resident(w_dec), *given)
    return codes, sums


def turn_kernel(chunk, *refs):
    *codes, out = refs
    for k, ref in enumerate(codes):
        lat = ref.shape[1]

        @pl.loop(0, lat // chunk)
        def _(i):
            at = pl.multiple_of(i * chunk, chunk)
            block = ref[:, pl.ds(at, chunk)].astype(jnp.float32).T
            out[pl.ds(k * lat + at, chunk), :] = block.astype(out.dtype)


def turn(*codes):
    tokens, lat = codes[0].shape
    return pl.pallas_call(
        functools.partial(turn_kernel, min(512, lat)),
        out_shape=jax.ShapeDtypeStruct((len(codes) * lat, tokens), codes[0].dtype),
        in_specs=[WHOLE] * len(codes),
        out_specs=WHOLE,
        cost_estimate=waits(4),
        compiler_params=params(8),
    )(*codes)


def sum_kernel(own, *refs):
    *terms, out = refs
    total = own[...]
    for ref in terms:
        total = total + ref[...]
    out[...] = total


def add_up(terms):
    return pl.pallas_call(
        sum_kernel,
        out_shape=jax.ShapeDtypeStruct(terms[0].shape, jnp.float32),
        in_specs=[WHOLE] * len(terms),
        out_specs=WHOLE,
        cost_estimate=waits(8),
        compiler_params=params(4),
    )(*terms)


def error_kernel(total, rows, *refs):
    *near, out = refs
    total = total[...]
    for ref in near:
        half = ref.shape[0] // 2
        total = total + jnp.concatenate([ref[half:], ref[:half]])
    out[...] = (total - rows[...].astype(jnp.float32)).astype(out.dtype)


def error(total, near, rows):
    return pl.pallas_call(
        error_kernel,
        out_shape=jax.ShapeDtypeStruct(rows.shape, rows.dtype),
        in_specs=[WHOLE] * (2 + len(near)),
        out_specs=WHOLE,
        cost_estimate=waits(8),
        compiler_params=params(4),
    )(total, rows, *near)


def reduce_rows(sums):
    if lax.axis_size("latent") > DIRECT:
        return lax.psum_scatter(sums[0], "latent", scatter_dimension=0, tiled=True), []
    terms = [sums[0]] + [swap(s, "latent", mask) for s, mask in zip(sums[1:], far_masks())]
    total = add_up(terms)
    return total, [swap(total, "latent", 1)]


def adam_kernel(codes_t, m, v, *refs):
    *blocks, out, even, odd, err = refs
    products = (even, odd)
    tokens = codes_t.shape[1]
    b = 0.1 / (1.0 - 0.9**10) / tokens
    a = 0.9 / (1.0 - 0.9**10) / b
    p = 0.999 / (1.0 - 0.999**10) / b**2
    q = 0.001 / (1.0 - 0.999**10) / tokens**2 / b**2
    a, p, q, eps = (jnp.asarray(x, out.dtype) for x in (a, p, q, 1e-8 / b))
    i, last = pl.program_id(0), pl.num_programs(0) - 1
    rows = out.shape[0]
    part = even.shape[0]
    slab, ahead = 16, 8
    slabs = part // slab

    def multiply(start):
        at = pl.ds(pl.multiple_of(start, part), part)
        c = jnp.dot(codes_t[at, :], err[...], preferred_element_type=jnp.float32)
        return c.astype(out.dtype)

    def direction(k, j):
        at = pl.ds(pl.multiple_of(i * rows + k * part + j * slab, slab), slab)
        c = products[k][j * slab : (j + 1) * slab, :]
        first = m[at, :] * a + c
        second = v[at, :] * p + (c * c) * q
        root = second * lax.rsqrt(second)
        return first * pl.reciprocal(root + eps, approx=True)

    @pl.when(i == 0)
    def _():
        err[...] = stack(blocks)
        even[...] = multiply(0)

    ready = []

    def store():
        at, step = ready.pop(0)
        out[at : at + slab, :] = step

    for k in range(2):
        later = multiply(i * rows + part if k == 0 else jnp.minimum(i + 1, last) * rows)
        into = products[1 - k]
        for j in range(slabs):
            ready.append((k * part + j * slab, direction(k, j)))
            if len(ready) > ahead:
                store()
            if 2 * j >= slabs:
                at = (2 * j - slabs) * slab
                into[at : at + 2 * slab, :] = later[at : at + 2 * slab]
    while ready:
        store()


def adam(codes_t, blocks, m, v):
    lat, half = m.shape
    rows = min(1024, lat)
    return pl.pallas_call(
        adam_kernel,
        grid=(lat // rows,),
        out_shape=jax.ShapeDtypeStruct(m.shape, jnp.bfloat16),
        in_specs=[WHOLE] * (3 + len(blocks)),
        out_specs=pl.BlockSpec((rows, half), lambda i: (i, 0)),
        scratch_shapes=[pltpu.VMEM((rows // 2, half), jnp.bfloat16)] * 2
        + [pltpu.VMEM((codes_t.shape[1], half), jnp.bfloat16)],
        compiler_params=params(12),
    )(codes_t, resident(m), resident(v), *blocks)


def per_device(acts, w_enc, b_enc, w_dec, dec_m, dec_v):
    direct = lax.axis_size("latent") <= DIRECT
    rows = near_rows(acts, 2 if direct else 1)
    blocks = spread(rows)
    part = w_enc.shape[1] // PARTS
    mine = [encode(blocks, w_enc, k * part, part) for k in range(PARTS)]
    theirs = [swap(x, "dp", 1) for x in mine]
    codes, sums = [], []
    for k in range(PARTS):
        far = len(blocks) if k == PARTS - 1 else 1
        block, sums = decode(mine[k], theirs[k], b_enc, w_dec, k * part, sums, far)
        codes.append(block)
    codes_t = turn(*codes)
    total, near = reduce_rows(sums)
    err = spread(error(total, near, rows))
    return adam(codes_t, err, dec_m, dec_v)


def solution(mesh):
    in_specs = (
        P(("groups", "latent", "dp"), None),
        P(("groups", "dp"), "latent"),
        P(("groups", "latent")),
        P(("groups", "latent"), "dp"),
        P(("groups", "latent"), "dp"),
        P(("groups", "latent"), "dp"),
    )
    out_specs = P(("groups", "latent"), "dp")
    return jax.shard_map(
        per_device, mesh=mesh, in_specs=in_specs, out_specs=out_specs, check_vma=False
    )
```

```python
import functools

import jax
import jax.numpy as jnp
from jax import lax
from jax.experimental import pallas as pl
from jax.experimental.pallas import tpu as pltpu
from jax.sharding import PartitionSpec as P

MIB = 1 << 20
PARTS = 2
WHOLE = pl.BlockSpec(memory_space=pltpu.VMEM)
DIRECT = 8


def swap(value, axis, mask):
    n = lax.axis_size(axis)
    return lax.ppermute(value, axis, [(i, i ^ mask) for i in range(n)])


def params(mib):
    return pltpu.CompilerParams(vmem_limit_bytes=mib * MIB)


def waits(mib):
    return pl.CostEstimate(flops=mib * 350_000_000, bytes_accessed=mib * MIB, transcendentals=0)


def resident(value):
    return pltpu.with_memory_space_constraint(value, pltpu.VMEM)


def far_masks():
    return range(2, lax.axis_size("latent"), 2)


def stack(refs):
    return jnp.concatenate([r[...].astype(jnp.float32) for r in refs]).astype(refs[0].dtype)


def near_kernel(*refs):
    *rows, out = refs
    half = out.shape[1]
    side = lax.axis_index("dp")

    def write(order, at):
        picked = [rows[i][:, at : at + half].astype(jnp.float32) for i in order]
        out[...] = jnp.concatenate(picked).astype(out.dtype)

    pairs = range(0, len(rows), 2)

    @pl.when(side == 0)
    def _():
        write([i + c for i in pairs for c in (0, 1)], 0)

    @pl.when(side == 1)
    def _():
        write([i + c for i in pairs for c in (1, 0)], half)


def copy_kernel(x, out):
    out[...] = x[...]


def near_rows(acts, near):
    axes = ("latent", "dp")
    own = pl.pallas_call(
        copy_kernel,
        out_shape=jax.ShapeDtypeStruct(acts.shape, acts.dtype),
        in_specs=[WHOLE],
        out_specs=WHOLE,
        cost_estimate=waits(1),
        compiler_params=params(4),
    )(acts)
    rows = [own] + [swap(acts, axes, mask) for mask in range(1, 2 * near)]
    return pl.pallas_call(
        near_kernel,
        out_shape=jax.ShapeDtypeStruct((len(rows) * acts.shape[0], acts.shape[1] // 2), acts.dtype),
        in_specs=[WHOLE] * len(rows),
        out_specs=WHOLE,
        cost_estimate=waits(14),
        compiler_params=params(4),
    )(*rows)


def spread(block):
    if lax.axis_size("latent") > DIRECT:
        return [lax.all_gather(block, "latent", axis=0, tiled=True)]
    return [block] + [swap(block, "latent", mask) for mask in far_masks()]


def encode_kernel(first, *refs):
    *rows_refs, w, out = refs
    lat = out.shape[1]
    out[...] = jnp.dot(
        stack(rows_refs), w[:, first : first + lat], preferred_element_type=jnp.float32
    )


def encode(blocks, w_enc, first, lat):
    tokens = sum(b.shape[0] for b in blocks)
    return pl.pallas_call(
        functools.partial(encode_kernel, first),
        out_shape=jax.ShapeDtypeStruct((tokens, lat), jnp.float32),
        in_specs=[WHOLE] * (len(blocks) + 1),
        out_specs=WHOLE,
        cost_estimate=waits(7),
        compiler_params=params(8),
    )(*blocks, resident(w_enc))


def decode_kernel(first, given, mine, theirs, bias, w, *refs):
    codes, *out = refs[given:]
    lat = mine.shape[1]
    pre = mine[...] + theirs[...] + bias[:, first : first + lat]
    block = jnp.maximum(pre, 0.0).astype(jnp.bfloat16)
    codes[...] = block
    total = jnp.dot(block, w[first : first + lat, :], preferred_element_type=jnp.float32)
    if given:
        total = total + refs[0][...]
    rows = out[0].shape[0]
    for j, ref in enumerate(out):
        ref[...] = total[j * rows : (j + 1) * rows].astype(ref.dtype)


def decode(mine, theirs, bias, w_dec, first, given, far):
    tokens, lat = mine.shape
    half = w_dec.shape[1]
    sums = [
        jax.ShapeDtypeStruct((tokens // far, half), jnp.bfloat16 if j else jnp.float32)
        for j in range(far)
    ]
    codes, *sums = pl.pallas_call(
        functools.partial(decode_kernel, first, len(given)),
        out_shape=[jax.ShapeDtypeStruct((tokens, lat), jnp.bfloat16)] + sums,
        in_specs=[WHOLE] * (4 + len(given)),
        out_specs=[WHOLE] * (1 + len(sums)),
        cost_estimate=waits(7),
        compiler_params=params(8),
    )(mine, theirs, bias.reshape(1, -1), resident(w_dec), *given)
    return codes, sums


def turn_kernel(chunk, *refs):
    *codes, out = refs
    for k, ref in enumerate(codes):
        lat = ref.shape[1]

        @pl.loop(0, lat // chunk)
        def _(i):
            at = pl.multiple_of(i * chunk, chunk)
            block = ref[:, pl.ds(at, chunk)].astype(jnp.float32).T
            out[pl.ds(k * lat + at, chunk), :] = block.astype(out.dtype)


def turn(*codes):
    tokens, lat = codes[0].shape
    return pl.pallas_call(
        functools.partial(turn_kernel, min(512, lat)),
        out_shape=jax.ShapeDtypeStruct((len(codes) * lat, tokens), codes[0].dtype),
        in_specs=[WHOLE] * len(codes),
        out_specs=WHOLE,
        cost_estimate=waits(4),
        compiler_params=params(8),
    )(*codes)


def sum_kernel(own, *refs):
    *terms, out = refs
    total = own[...]
    for ref in terms:
        total = total + ref[...]
    out[...] = total


def add_up(terms):
    return pl.pallas_call(
        sum_kernel,
        out_shape=jax.ShapeDtypeStruct(terms[0].shape, jnp.float32),
        in_specs=[WHOLE] * len(terms),
        out_specs=WHOLE,
        cost_estimate=waits(8),
        compiler_params=params(4),
    )(*terms)


def error_kernel(total, rows, *refs):
    *near, out = refs
    total = total[...]
    for ref in near:
        half = ref.shape[0] // 2
        total = total + jnp.concatenate([ref[half:], ref[:half]])
    out[...] = (total - rows[...].astype(jnp.float32)).astype(out.dtype)


def error(total, near, rows):
    return pl.pallas_call(
        error_kernel,
        out_shape=jax.ShapeDtypeStruct(rows.shape, rows.dtype),
        in_specs=[WHOLE] * (2 + len(near)),
        out_specs=WHOLE,
        cost_estimate=waits(8),
        compiler_params=params(4),
    )(total, rows, *near)


def reduce_rows(sums):
    if lax.axis_size("latent") > DIRECT:
        return lax.psum_scatter(sums[0], "latent", scatter_dimension=0, tiled=True), []
    terms = [sums[0]] + [swap(s, "latent", mask) for s, mask in zip(sums[1:], far_masks())]
    total = add_up(terms)
    return total, [swap(total, "latent", 1)]


def adam_kernel(codes_t, m, v, *refs):
    *blocks, out, even, odd, err, ready, sems = refs
    products = (even, odd)
    tokens = codes_t.shape[1]
    b = 0.1 / (1.0 - 0.9**10) / tokens
    a = 0.9 / (1.0 - 0.9**10) / b
    p = 0.999 / (1.0 - 0.999**10) / b**2
    q = 0.001 / (1.0 - 0.999**10) / tokens**2 / b**2
    a, p, q, eps = (jnp.asarray(x, out.dtype) for x in (a, p, q, 1e-8 / b))
    i, steps = pl.program_id(0), pl.num_programs(0)
    rows, half = ready.shape[1:]
    part = even.shape[0]
    pieces = sems.shape[1]
    piece = rows // pieces
    slab = 16
    slot = lax.rem(i, 2)

    def sent(step, k):
        slot = lax.rem(step, 2)
        at = pl.ds(pl.multiple_of(step * rows + k * piece, piece), piece)
        return pltpu.make_async_copy(
            ready.at[slot, pl.ds(k * piece, piece)], out.at[at], sems.at[slot, k]
        )

    def multiply(start, product):
        at = pl.ds(pl.multiple_of(start, part), part)
        c = jnp.dot(codes_t[at, :], err[...], preferred_element_type=jnp.float32)
        product[...] = c.astype(product.dtype)

    @pl.when(i == 0)
    def _():
        err[...] = stack(blocks)
        multiply(0, even)

    @pl.when(i >= 2)
    def _():
        for k in range(pieces):
            sent(i - 2, k).wait()

    for r in range(0, rows, slab):
        if r == 0:
            multiply(i * rows + part, odd)
        if r == part:
            multiply(jnp.minimum(i + 1, steps - 1) * rows, even)
        at = pl.ds(pl.multiple_of(i * rows + r, slab), slab)
        c = products[r // part][r % part : r % part + slab, :]
        first = m[at, :] * a + c
        second = v[at, :] * p + (c * c) * q
        root = second * lax.rsqrt(second)
        step = first * pl.reciprocal(root + eps, approx=True)
        ready[slot, r : r + slab, :] = step
        if (r + slab) % piece == 0:
            sent(i, r // piece).start()

    @pl.when(i == steps - 1)
    def _():
        for k in range(pieces):
            sent(i, k).wait()

    @pl.when((i == steps - 1) & (i >= 1))
    def _():
        for k in range(pieces):
            sent(i - 1, k).wait()


def adam(codes_t, blocks, m, v):
    lat, half = m.shape
    rows = min(1024, lat)
    return pl.pallas_call(
        adam_kernel,
        grid=(lat // rows,),
        out_shape=jax.ShapeDtypeStruct(m.shape, jnp.bfloat16),
        in_specs=[WHOLE] * (3 + len(blocks)),
        out_specs=pl.BlockSpec(memory_space=pl.ANY),
        scratch_shapes=[pltpu.VMEM((rows // 2, half), jnp.bfloat16)] * 2
        + [
            pltpu.VMEM((codes_t.shape[1], half), jnp.bfloat16),
            pltpu.VMEM((2, rows, half), jnp.bfloat16),
            pltpu.SemaphoreType.DMA((2, 4)),
        ],
        compiler_params=params(12),
    )(codes_t, resident(m), resident(v), *blocks)


def per_device(acts, w_enc, b_enc, w_dec, dec_m, dec_v):
    direct = lax.axis_size("latent") <= DIRECT
    rows = near_rows(acts, 2 if direct else 1)
    blocks = spread(rows)
    part = w_enc.shape[1] // PARTS
    mine = [encode(blocks, w_enc, k * part, part) for k in range(PARTS)]
    theirs = [swap(x, "dp", 1) for x in mine]
    codes, sums = [], []
    for k in range(PARTS):
        far = len(blocks) if k == PARTS - 1 else 1
        block, sums = decode(mine[k], theirs[k], b_enc, w_dec, k * part, sums, far)
        codes.append(block)
    codes_t = turn(*codes)
    total, near = reduce_rows(sums)
    err = spread(error(total, near, rows))
    return adam(codes_t, err, dec_m, dec_v)


def solution(mesh):
    in_specs = (
        P(("groups", "latent", "dp"), None),
        P(("groups", "dp"), "latent"),
        P(("groups", "latent")),
        P(("groups", "latent"), "dp"),
        P(("groups", "latent"), "dp"),
        P(("groups", "latent"), "dp"),
    )
    out_specs = P(("groups", "latent"), "dp")
    return jax.shard_map(
        per_device, mesh=mesh, in_specs=in_specs, out_specs=out_specs, check_vma=False
    )
```

```python
import functools

import jax
import jax.numpy as jnp
from jax import lax
from jax.experimental import pallas as pl
from jax.experimental.pallas import tpu as pltpu
from jax.sharding import PartitionSpec as P

MIB = 1 << 20
PARTS = 2
WHOLE = pl.BlockSpec(memory_space=pltpu.VMEM)
DIRECT = 8


def swap(value, axis, mask):
    n = lax.axis_size(axis)
    return lax.ppermute(value, axis, [(i, i ^ mask) for i in range(n)])


def params(mib):
    return pltpu.CompilerParams(vmem_limit_bytes=mib * MIB)


def waits(mib):
    return pl.CostEstimate(flops=mib * 350_000_000, bytes_accessed=mib * MIB, transcendentals=0)


def resident(value):
    return pltpu.with_memory_space_constraint(value, pltpu.VMEM)


def far_masks():
    return range(2, lax.axis_size("latent"), 2)


def stack(refs):
    return jnp.concatenate([r[...].astype(jnp.float32) for r in refs]).astype(refs[0].dtype)


def near_kernel(*refs):
    *rows, out = refs
    half = out.shape[1]
    side = lax.axis_index("dp")

    def write(order, at):
        picked = [rows[i][:, at : at + half].astype(jnp.float32) for i in order]
        out[...] = jnp.concatenate(picked).astype(out.dtype)

    pairs = range(0, len(rows), 2)

    @pl.when(side == 0)
    def _():
        write([i + c for i in pairs for c in (0, 1)], 0)

    @pl.when(side == 1)
    def _():
        write([i + c for i in pairs for c in (1, 0)], half)


def copy_kernel(x, out):
    out[...] = x[...]


def near_rows(acts, near):
    axes = ("latent", "dp")
    own = pl.pallas_call(
        copy_kernel,
        out_shape=jax.ShapeDtypeStruct(acts.shape, acts.dtype),
        in_specs=[WHOLE],
        out_specs=WHOLE,
        cost_estimate=waits(1),
        compiler_params=params(4),
    )(acts)
    rows = [own] + [swap(acts, axes, mask) for mask in range(1, 2 * near)]
    return pl.pallas_call(
        near_kernel,
        out_shape=jax.ShapeDtypeStruct((len(rows) * acts.shape[0], acts.shape[1] // 2), acts.dtype),
        in_specs=[WHOLE] * len(rows),
        out_specs=WHOLE,
        cost_estimate=waits(14),
        compiler_params=params(4),
    )(*rows)


def spread(block):
    if lax.axis_size("latent") > DIRECT:
        return [lax.all_gather(block, "latent", axis=0, tiled=True)]
    return [block] + [swap(block, "latent", mask) for mask in far_masks()]


def encode_kernel(first, *refs):
    *rows_refs, w, out = refs
    lat = out.shape[1]
    out[...] = jnp.dot(
        stack(rows_refs), w[:, first : first + lat], preferred_element_type=jnp.float32
    )


def encode(blocks, w_enc, first, lat):
    tokens = sum(b.shape[0] for b in blocks)
    return pl.pallas_call(
        functools.partial(encode_kernel, first),
        out_shape=jax.ShapeDtypeStruct((tokens, lat), jnp.float32),
        in_specs=[WHOLE] * (len(blocks) + 1),
        out_specs=WHOLE,
        cost_estimate=waits(7),
        compiler_params=params(8),
    )(*blocks, resident(w_enc))


def decode_kernel(first, given, mine, theirs, bias, w, *refs):
    codes, *out = refs[given:]
    lat = mine.shape[1]
    pre = mine[...] + theirs[...] + bias[:, first : first + lat]
    block = jnp.maximum(pre, 0.0).astype(jnp.bfloat16)
    codes[...] = block
    total = jnp.dot(block, w[first : first + lat, :], preferred_element_type=jnp.float32)
    if given:
        total = total + refs[0][...]
    rows = out[0].shape[0]
    for j, ref in enumerate(out):
        ref[...] = total[j * rows : (j + 1) * rows].astype(ref.dtype)


def decode(mine, theirs, bias, w_dec, first, given, far):
    tokens, lat = mine.shape
    half = w_dec.shape[1]
    sums = [
        jax.ShapeDtypeStruct((tokens // far, half), jnp.bfloat16 if j else jnp.float32)
        for j in range(far)
    ]
    codes, *sums = pl.pallas_call(
        functools.partial(decode_kernel, first, len(given)),
        out_shape=[jax.ShapeDtypeStruct((tokens, lat), jnp.bfloat16)] + sums,
        in_specs=[WHOLE] * (4 + len(given)),
        out_specs=[WHOLE] * (1 + len(sums)),
        cost_estimate=waits(7),
        compiler_params=params(8),
    )(mine, theirs, bias.reshape(1, -1), resident(w_dec), *given)
    return codes, sums


def turn_kernel(chunk, *refs):
    *codes, out = refs
    for k, ref in enumerate(codes):
        lat = ref.shape[1]

        @pl.loop(0, lat // chunk)
        def _(i):
            at = pl.multiple_of(i * chunk, chunk)
            block = ref[:, pl.ds(at, chunk)].astype(jnp.float32).T
            out[pl.ds(k * lat + at, chunk), :] = block.astype(out.dtype)


def turn(*codes):
    tokens, lat = codes[0].shape
    return pl.pallas_call(
        functools.partial(turn_kernel, min(512, lat)),
        out_shape=jax.ShapeDtypeStruct((len(codes) * lat, tokens), codes[0].dtype),
        in_specs=[WHOLE] * len(codes),
        out_specs=WHOLE,
        cost_estimate=waits(4),
        compiler_params=params(8),
    )(*codes)


def sum_kernel(own, *refs):
    *terms, out = refs
    total = own[...]
    for ref in terms:
        total = total + ref[...]
    out[...] = total


def add_up(terms):
    return pl.pallas_call(
        sum_kernel,
        out_shape=jax.ShapeDtypeStruct(terms[0].shape, jnp.float32),
        in_specs=[WHOLE] * len(terms),
        out_specs=WHOLE,
        cost_estimate=waits(8),
        compiler_params=params(4),
    )(*terms)


def error_kernel(total, rows, *refs):
    *near, out = refs
    total = total[...]
    for ref in near:
        half = ref.shape[0] // 2
        total = total + jnp.concatenate([ref[half:], ref[:half]])
    out[...] = (total - rows[...].astype(jnp.float32)).astype(out.dtype)


def error(total, near, rows):
    return pl.pallas_call(
        error_kernel,
        out_shape=jax.ShapeDtypeStruct(rows.shape, rows.dtype),
        in_specs=[WHOLE] * (2 + len(near)),
        out_specs=WHOLE,
        cost_estimate=waits(8),
        compiler_params=params(4),
    )(total, rows, *near)


def reduce_rows(sums):
    if lax.axis_size("latent") > DIRECT:
        return lax.psum_scatter(sums[0], "latent", scatter_dimension=0, tiled=True), []
    terms = [sums[0]] + [swap(s, "latent", mask) for s, mask in zip(sums[1:], far_masks())]
    total = add_up(terms)
    return total, [swap(total, "latent", 1)]


def adam_kernel(codes_t, m, v, *refs):
    *blocks, out, even, odd, err = refs
    products = (even, odd)
    tokens = codes_t.shape[1]
    b = 0.1 / (1.0 - 0.9**10) / tokens
    a = 0.9 / 0.1 * tokens
    p = 0.999 / 0.001 * tokens**2
    scale = b / (0.001 / (1.0 - 0.999**10) / tokens**2) ** 0.5
    eps = 1e-8 / b * scale**2
    a, p, scale, eps = (jnp.asarray(x, out.dtype) for x in (a, p, scale, eps))
    i, last = pl.program_id(0), pl.num_programs(0) - 1
    rows = out.shape[0]
    part = even.shape[0]
    slab = 16

    def multiply(start, product):
        at = pl.ds(pl.multiple_of(start, part), part)
        c = jnp.dot(codes_t[at, :], err[...], preferred_element_type=jnp.float32)
        product[...] = c.astype(product.dtype)

    @pl.when(i == 0)
    def _():
        err[...] = stack(blocks)
        multiply(0, even)

    for k in range(2):
        if k == 0:
            multiply(i * rows + part, odd)
        else:
            multiply(jnp.minimum(i + 1, last) * rows, even)
        for r in range(0, part, slab):
            at = pl.ds(pl.multiple_of(i * rows + k * part + r, slab), slab)
            c = products[k][r : r + slab, :]
            first = m[at, :] * a + c
            second = v[at, :] * p + c * c
            inverse = lax.rsqrt(second)
            step = first * (inverse * (scale - inverse * eps))
            out[k * part + r : k * part + r + slab, :] = step


def adam(codes_t, blocks, m, v):
    lat, half = m.shape
    rows = min(1024, lat)
    return pl.pallas_call(
        adam_kernel,
        grid=(lat // rows,),
        out_shape=jax.ShapeDtypeStruct(m.shape, jnp.bfloat16),
        in_specs=[WHOLE] * (3 + len(blocks)),
        out_specs=pl.BlockSpec((rows, half), lambda i: (i, 0)),
        scratch_shapes=[pltpu.VMEM((rows // 2, half), jnp.bfloat16)] * 2
        + [pltpu.VMEM((codes_t.shape[1], half), jnp.bfloat16)],
        compiler_params=params(12),
    )(codes_t, resident(m), resident(v), *blocks)


def per_device(acts, w_enc, b_enc, w_dec, dec_m, dec_v):
    direct = lax.axis_size("latent") <= DIRECT
    rows = near_rows(acts, 2 if direct else 1)
    blocks = spread(rows)
    part = w_enc.shape[1] // PARTS
    mine = [encode(blocks, w_enc, k * part, part) for k in range(PARTS)]
    theirs = [swap(x, "dp", 1) for x in mine]
    codes, sums = [], []
    for k in range(PARTS):
        far = len(blocks) if k == PARTS - 1 else 1
        block, sums = decode(mine[k], theirs[k], b_enc, w_dec, k * part, sums, far)
        codes.append(block)
    codes_t = turn(*codes)
    total, near = reduce_rows(sums)
    err = spread(error(total, near, rows))
    return adam(codes_t, err, dec_m, dec_v)


def solution(mesh):
    in_specs = (
        P(("groups", "latent", "dp"), None),
        P(("groups", "dp"), "latent"),
        P(("groups", "latent")),
        P(("groups", "latent"), "dp"),
        P(("groups", "latent"), "dp"),
        P(("groups", "latent"), "dp"),
    )
    out_specs = P(("groups", "latent"), "dp")
    return jax.shard_map(
        per_device, mesh=mesh, in_specs=in_specs, out_specs=out_specs, check_vma=False
    )
```

```python
import functools

import jax
import jax.numpy as jnp
from jax import lax
from jax.experimental import pallas as pl
from jax.experimental.pallas import tpu as pltpu
from jax.sharding import PartitionSpec as P

MIB = 1 << 20
PARTS = 2
WHOLE = pl.BlockSpec(memory_space=pltpu.VMEM)
DIRECT = 8


def swap(value, axis, mask):
    n = lax.axis_size(axis)
    return lax.ppermute(value, axis, [(i, i ^ mask) for i in range(n)])


def params(mib):
    return pltpu.CompilerParams(vmem_limit_bytes=mib * MIB)


def waits(mib):
    return pl.CostEstimate(flops=mib * 350_000_000, bytes_accessed=mib * MIB, transcendentals=0)


def resident(value):
    return pltpu.with_memory_space_constraint(value, pltpu.VMEM)


def far_masks():
    return range(2, lax.axis_size("latent"), 2)


def stack(refs):
    return jnp.concatenate([r[...].astype(jnp.float32) for r in refs]).astype(refs[0].dtype)


def near_kernel(*refs):
    *rows, out = refs
    half = out.shape[1]
    side = lax.axis_index("dp")

    def write(order, at):
        picked = [rows[i][:, at : at + half].astype(jnp.float32) for i in order]
        out[...] = jnp.concatenate(picked).astype(out.dtype)

    pairs = range(0, len(rows), 2)

    @pl.when(side == 0)
    def _():
        write([i + c for i in pairs for c in (0, 1)], 0)

    @pl.when(side == 1)
    def _():
        write([i + c for i in pairs for c in (1, 0)], half)


def copy_kernel(x, out):
    out[...] = x[...]


def near_rows(acts, near):
    axes = ("latent", "dp")
    own = pl.pallas_call(
        copy_kernel,
        out_shape=jax.ShapeDtypeStruct(acts.shape, acts.dtype),
        in_specs=[WHOLE],
        out_specs=WHOLE,
        cost_estimate=waits(1),
        compiler_params=params(4),
    )(acts)
    rows = [own] + [swap(acts, axes, mask) for mask in range(1, 2 * near)]
    return pl.pallas_call(
        near_kernel,
        out_shape=jax.ShapeDtypeStruct((len(rows) * acts.shape[0], acts.shape[1] // 2), acts.dtype),
        in_specs=[WHOLE] * len(rows),
        out_specs=WHOLE,
        cost_estimate=waits(14),
        compiler_params=params(4),
    )(*rows)


def spread(block):
    if lax.axis_size("latent") > DIRECT:
        return [lax.all_gather(block, "latent", axis=0, tiled=True)]
    return [block] + [swap(block, "latent", mask) for mask in far_masks()]


def encode_kernel(first, *refs):
    *rows_refs, w, out = refs
    lat = out.shape[1]
    out[...] = jnp.dot(
        stack(rows_refs), w[:, first : first + lat], preferred_element_type=jnp.float32
    )


def encode(blocks, w_enc, first, lat):
    tokens = sum(b.shape[0] for b in blocks)
    return pl.pallas_call(
        functools.partial(encode_kernel, first),
        out_shape=jax.ShapeDtypeStruct((tokens, lat), jnp.float32),
        in_specs=[WHOLE] * (len(blocks) + 1),
        out_specs=WHOLE,
        cost_estimate=waits(7),
        compiler_params=params(8),
    )(*blocks, resident(w_enc))


def decode_kernel(first, given, mine, theirs, bias, w, *refs):
    codes, *out = refs[given:]
    lat = mine.shape[1]
    pre = mine[...] + theirs[...] + bias[:, first : first + lat]
    block = jnp.maximum(pre, 0.0).astype(jnp.bfloat16)
    codes[...] = block
    total = jnp.dot(block, w[first : first + lat, :], preferred_element_type=jnp.float32)
    if given:
        total = total + refs[0][...]
    rows = out[0].shape[0]
    for j, ref in enumerate(out):
        ref[...] = total[j * rows : (j + 1) * rows].astype(ref.dtype)


def decode(mine, theirs, bias, w_dec, first, given, far):
    tokens, lat = mine.shape
    half = w_dec.shape[1]
    sums = [
        jax.ShapeDtypeStruct((tokens // far, half), jnp.bfloat16 if j else jnp.float32)
        for j in range(far)
    ]
    codes, *sums = pl.pallas_call(
        functools.partial(decode_kernel, first, len(given)),
        out_shape=[jax.ShapeDtypeStruct((tokens, lat), jnp.bfloat16)] + sums,
        in_specs=[WHOLE] * (4 + len(given)),
        out_specs=[WHOLE] * (1 + len(sums)),
        cost_estimate=waits(7),
        compiler_params=params(8),
    )(mine, theirs, bias.reshape(1, -1), resident(w_dec), *given)
    return codes, sums


def turn_kernel(chunk, *refs):
    *codes, out = refs
    for k, ref in enumerate(codes):
        lat = ref.shape[1]

        @pl.loop(0, lat // chunk)
        def _(i):
            at = pl.multiple_of(i * chunk, chunk)
            block = ref[:, pl.ds(at, chunk)].astype(jnp.float32).T
            out[pl.ds(k * lat + at, chunk), :] = block.astype(out.dtype)


def turn(*codes):
    tokens, lat = codes[0].shape
    return pl.pallas_call(
        functools.partial(turn_kernel, min(512, lat)),
        out_shape=jax.ShapeDtypeStruct((len(codes) * lat, tokens), codes[0].dtype),
        in_specs=[WHOLE] * len(codes),
        out_specs=WHOLE,
        cost_estimate=waits(4),
        compiler_params=params(8),
    )(*codes)


def sum_kernel(own, *refs):
    *terms, out = refs
    total = own[...]
    for ref in terms:
        total = total + ref[...]
    out[...] = total


def add_up(terms):
    return pl.pallas_call(
        sum_kernel,
        out_shape=jax.ShapeDtypeStruct(terms[0].shape, jnp.float32),
        in_specs=[WHOLE] * len(terms),
        out_specs=WHOLE,
        cost_estimate=waits(8),
        compiler_params=params(4),
    )(*terms)


def error_kernel(factor, total, rows, *refs):
    *near, out = refs
    total = total[...]
    for ref in near:
        half = ref.shape[0] // 2
        total = total + jnp.concatenate([ref[half:], ref[:half]])
    out[...] = ((total - rows[...].astype(jnp.float32)) * factor).astype(out.dtype)


def error(total, near, rows, factor):
    return pl.pallas_call(
        functools.partial(error_kernel, factor),
        out_shape=jax.ShapeDtypeStruct(rows.shape, rows.dtype),
        in_specs=[WHOLE] * (2 + len(near)),
        out_specs=WHOLE,
        cost_estimate=waits(8),
        compiler_params=params(4),
    )(total, rows, *near)


def reduce_rows(sums):
    if lax.axis_size("latent") > DIRECT:
        return lax.psum_scatter(sums[0], "latent", scatter_dimension=0, tiled=True), []
    terms = [sums[0]] + [swap(s, "latent", mask) for s, mask in zip(sums[1:], far_masks())]
    total = add_up(terms)
    return total, [swap(total, "latent", 1)]


def adam_kernel(codes_t, m, v, *refs):
    *blocks, out, even, odd, err = refs
    products = (even, odd)
    b1, b2 = 1.0 - 0.9**10, 1.0 - 0.999**10
    p = 0.999 / 0.081
    scale = 0.9 / b1 / (0.081 / b2) ** 0.5
    eps = 1e-8 / (0.9 / b1) * scale**2
    p, scale, eps = (jnp.asarray(x, out.dtype) for x in (p, scale, eps))
    i, last = pl.program_id(0), pl.num_programs(0) - 1
    rows = out.shape[0]
    part = even.shape[0]
    slab = 16

    def multiply(start, product):
        at = pl.ds(pl.multiple_of(start, part), part)
        c = jnp.dot(codes_t[at, :], err[...], preferred_element_type=jnp.float32)
        product[...] = c.astype(product.dtype)

    @pl.when(i == 0)
    def _():
        err[...] = stack(blocks)
        multiply(0, even)

    for k in range(2):
        if k == 0:
            multiply(i * rows + part, odd)
        else:
            multiply(jnp.minimum(i + 1, last) * rows, even)
        for r in range(0, part, slab):
            at = pl.ds(pl.multiple_of(i * rows + k * part + r, slab), slab)
            c = products[k][r : r + slab, :]
            first = m[at, :] + c
            second = v[at, :] * p + c * c
            inverse = lax.rsqrt(second)
            step = first * (inverse * (scale - inverse * eps))
            out[k * part + r : k * part + r + slab, :] = step


def adam(codes_t, blocks, m, v):
    lat, half = m.shape
    rows = min(1024, lat)
    return pl.pallas_call(
        adam_kernel,
        grid=(lat // rows,),
        out_shape=jax.ShapeDtypeStruct(m.shape, jnp.bfloat16),
        in_specs=[WHOLE] * (3 + len(blocks)),
        out_specs=pl.BlockSpec((rows, half), lambda i: (i, 0)),
        scratch_shapes=[pltpu.VMEM((rows // 2, half), jnp.bfloat16)] * 2
        + [pltpu.VMEM((codes_t.shape[1], half), jnp.bfloat16)],
        compiler_params=params(12),
    )(codes_t, resident(m), resident(v), *blocks)


def per_device(acts, w_enc, b_enc, w_dec, dec_m, dec_v):
    direct = lax.axis_size("latent") <= DIRECT
    rows = near_rows(acts, 2 if direct else 1)
    blocks = spread(rows)
    part = w_enc.shape[1] // PARTS
    mine = [encode(blocks, w_enc, k * part, part) for k in range(PARTS)]
    theirs = [swap(x, "dp", 1) for x in mine]
    codes, sums = [], []
    for k in range(PARTS):
        far = len(blocks) if k == PARTS - 1 else 1
        block, sums = decode(mine[k], theirs[k], b_enc, w_dec, k * part, sums, far)
        codes.append(block)
    codes_t = turn(*codes)
    total, near = reduce_rows(sums)
    factor = 0.1 / 0.9 / codes_t.shape[1]
    err = spread(error(total, near, rows, factor))
    return adam(codes_t, err, dec_m, dec_v)


def solution(mesh):
    in_specs = (
        P(("groups", "latent", "dp"), None),
        P(("groups", "dp"), "latent"),
        P(("groups", "latent")),
        P(("groups", "latent"), "dp"),
        P(("groups", "latent"), "dp"),
        P(("groups", "latent"), "dp"),
    )
    out_specs = P(("groups", "latent"), "dp")
    return jax.shard_map(
        per_device, mesh=mesh, in_specs=in_specs, out_specs=out_specs, check_vma=False
    )
```

```python
import functools

import jax
import jax.numpy as jnp
from jax import lax
from jax.experimental import pallas as pl
from jax.experimental.pallas import tpu as pltpu
from jax.sharding import PartitionSpec as P

MIB = 1 << 20
PARTS = 2
WHOLE = pl.BlockSpec(memory_space=pltpu.VMEM)
DIRECT = 8


def swap(value, axis, mask):
    n = lax.axis_size(axis)
    return lax.ppermute(value, axis, [(i, i ^ mask) for i in range(n)])


def params(mib):
    return pltpu.CompilerParams(vmem_limit_bytes=mib * MIB)


def waits(mib):
    return pl.CostEstimate(flops=mib * 350_000_000, bytes_accessed=mib * MIB, transcendentals=0)


def resident(value):
    return pltpu.with_memory_space_constraint(value, pltpu.VMEM)


def far_masks():
    return range(2, lax.axis_size("latent"), 2)


def stack(refs):
    return jnp.concatenate([r[...].astype(jnp.float32) for r in refs]).astype(refs[0].dtype)


def near_kernel(*refs):
    *rows, out = refs
    half = out.shape[1]
    side = lax.axis_index("dp")

    def write(order, at):
        picked = [rows[i][:, at : at + half].astype(jnp.float32) for i in order]
        out[...] = jnp.concatenate(picked).astype(out.dtype)

    pairs = range(0, len(rows), 2)

    @pl.when(side == 0)
    def _():
        write([i + c for i in pairs for c in (0, 1)], 0)

    @pl.when(side == 1)
    def _():
        write([i + c for i in pairs for c in (1, 0)], half)


def copy_kernel(x, out):
    out[...] = x[...]


def near_rows(acts, near):
    axes = ("latent", "dp")
    own = pl.pallas_call(
        copy_kernel,
        out_shape=jax.ShapeDtypeStruct(acts.shape, acts.dtype),
        in_specs=[WHOLE],
        out_specs=WHOLE,
        cost_estimate=waits(1),
        compiler_params=params(4),
    )(acts)
    rows = [own] + [swap(acts, axes, mask) for mask in range(1, 2 * near)]
    return pl.pallas_call(
        near_kernel,
        out_shape=jax.ShapeDtypeStruct((len(rows) * acts.shape[0], acts.shape[1] // 2), acts.dtype),
        in_specs=[WHOLE] * len(rows),
        out_specs=WHOLE,
        cost_estimate=waits(14),
        compiler_params=params(4),
    )(*rows)


def spread(block):
    if lax.axis_size("latent") > DIRECT:
        return [lax.all_gather(block, "latent", axis=0, tiled=True)]
    return [block] + [swap(block, "latent", mask) for mask in far_masks()]


def encode_kernel(first, *refs):
    *rows_refs, w, out = refs
    lat = out.shape[1]
    out[...] = jnp.dot(
        stack(rows_refs), w[:, first : first + lat], preferred_element_type=jnp.float32
    )


def encode(blocks, w_enc, first, lat):
    tokens = sum(b.shape[0] for b in blocks)
    return pl.pallas_call(
        functools.partial(encode_kernel, first),
        out_shape=jax.ShapeDtypeStruct((tokens, lat), jnp.float32),
        in_specs=[WHOLE] * (len(blocks) + 1),
        out_specs=WHOLE,
        cost_estimate=waits(7),
        compiler_params=params(8),
    )(*blocks, resident(w_enc))


def decode_kernel(first, given, mine, theirs, bias, w, *refs):
    codes, *out = refs[given:]
    lat = mine.shape[1]
    pre = mine[...] + theirs[...] + bias[:, first : first + lat]
    block = jnp.maximum(pre, 0.0).astype(jnp.bfloat16)
    codes[...] = block
    total = jnp.dot(block, w[first : first + lat, :], preferred_element_type=jnp.float32)
    if given:
        total = total + refs[0][...]
    rows = out[0].shape[0]
    for j, ref in enumerate(out):
        ref[...] = total[j * rows : (j + 1) * rows].astype(ref.dtype)


def decode(mine, theirs, bias, w_dec, first, given, far):
    tokens, lat = mine.shape
    half = w_dec.shape[1]
    sums = [
        jax.ShapeDtypeStruct((tokens // far, half), jnp.bfloat16 if j else jnp.float32)
        for j in range(far)
    ]
    codes, *sums = pl.pallas_call(
        functools.partial(decode_kernel, first, len(given)),
        out_shape=[jax.ShapeDtypeStruct((tokens, lat), jnp.bfloat16)] + sums,
        in_specs=[WHOLE] * (4 + len(given)),
        out_specs=[WHOLE] * (1 + len(sums)),
        cost_estimate=waits(7),
        compiler_params=params(8),
    )(mine, theirs, bias.reshape(1, -1), resident(w_dec), *given)
    return codes, sums


def turn_kernel(chunk, *refs):
    *codes, out = refs
    for k, ref in enumerate(codes):
        lat = ref.shape[1]

        @pl.loop(0, lat // chunk)
        def _(i):
            at = pl.multiple_of(i * chunk, chunk)
            block = ref[:, pl.ds(at, chunk)].astype(jnp.float32).T
            out[pl.ds(k * lat + at, chunk), :] = block.astype(out.dtype)


def turn(*codes):
    tokens, lat = codes[0].shape
    return pl.pallas_call(
        functools.partial(turn_kernel, min(512, lat)),
        out_shape=jax.ShapeDtypeStruct((len(codes) * lat, tokens), codes[0].dtype),
        in_specs=[WHOLE] * len(codes),
        out_specs=WHOLE,
        cost_estimate=waits(4),
        compiler_params=params(8),
    )(*codes)


def sum_kernel(own, *refs):
    *terms, out = refs
    total = own[...]
    for ref in terms:
        total = total + ref[...]
    out[...] = total


def add_up(terms):
    return pl.pallas_call(
        sum_kernel,
        out_shape=jax.ShapeDtypeStruct(terms[0].shape, jnp.float32),
        in_specs=[WHOLE] * len(terms),
        out_specs=WHOLE,
        cost_estimate=waits(8),
        compiler_params=params(4),
    )(*terms)


def error_kernel(factor, total, rows, *refs):
    *near, out = refs
    total = total[...]
    for ref in near:
        half = ref.shape[0] // 2
        total = total + jnp.concatenate([ref[half:], ref[:half]])
    out[...] = ((total - rows[...].astype(jnp.float32)) * factor).astype(out.dtype)


def error(total, near, rows, factor):
    return pl.pallas_call(
        functools.partial(error_kernel, factor),
        out_shape=jax.ShapeDtypeStruct(rows.shape, rows.dtype),
        in_specs=[WHOLE] * (2 + len(near)),
        out_specs=WHOLE,
        cost_estimate=waits(8),
        compiler_params=params(4),
    )(total, rows, *near)


def reduce_rows(sums):
    if lax.axis_size("latent") > DIRECT:
        return lax.psum_scatter(sums[0], "latent", scatter_dimension=0, tiled=True), []
    terms = [sums[0]] + [swap(s, "latent", mask) for s, mask in zip(sums[1:], far_masks())]
    total = add_up(terms)
    return total, [swap(total, "latent", 1)]


def adam_kernel(codes_t, m, v, *refs):
    *blocks, out, even, odd, err = refs
    products = (even, odd)
    b1, b2 = 1.0 - 0.9**10, 1.0 - 0.999**10
    p = 0.999 / 0.081
    scale = 0.9 / b1 / (0.081 / b2) ** 0.5
    eps = 1e-8 / (0.9 / b1) * scale**2
    p, scale, eps = (jnp.asarray(x, out.dtype) for x in (p, scale, eps))
    i, last = pl.program_id(0), pl.num_programs(0) - 1
    rows = out.shape[0]
    part = even.shape[0]
    slab, group = 32, part // 2

    def multiply(start, product, g):
        at = pl.ds(pl.multiple_of(start + g, group), group)
        c = jnp.dot(codes_t[at, :], err[...], preferred_element_type=jnp.float32)
        product[g : g + group, :] = c.astype(product.dtype)

    @pl.when(i == 0)
    def _():
        err[...] = stack(blocks)
        for g in range(0, part, group):
            multiply(0, even, g)

    for k in range(2):
        for r in range(0, part, slab):
            if r % group == 0 and k == 0:
                multiply(i * rows + part, odd, r)
            elif r % group == 0:
                multiply(jnp.minimum(i + 1, last) * rows, even, r)
            at = pl.ds(pl.multiple_of(i * rows + k * part + r, slab), slab)
            c = products[k][r : r + slab, :]
            first = m[at, :] + c
            second = v[at, :] * p + c * c
            inverse = lax.rsqrt(second)
            step = first * (inverse * (scale - inverse * eps))
            out[k * part + r : k * part + r + slab, :] = step


def adam(codes_t, blocks, m, v):
    lat, half = m.shape
    rows = min(1024, lat)
    return pl.pallas_call(
        adam_kernel,
        grid=(lat // rows,),
        out_shape=jax.ShapeDtypeStruct(m.shape, jnp.bfloat16),
        in_specs=[WHOLE] * (3 + len(blocks)),
        out_specs=pl.BlockSpec((rows, half), lambda i: (i, 0)),
        scratch_shapes=[pltpu.VMEM((rows // 2, half), jnp.bfloat16)] * 2
        + [pltpu.VMEM((codes_t.shape[1], half), jnp.bfloat16)],
        compiler_params=params(12),
    )(codes_t, resident(m), resident(v), *blocks)


def per_device(acts, w_enc, b_enc, w_dec, dec_m, dec_v):
    direct = lax.axis_size("latent") <= DIRECT
    rows = near_rows(acts, 2 if direct else 1)
    blocks = spread(rows)
    part = w_enc.shape[1] // PARTS
    mine = [encode(blocks, w_enc, k * part, part) for k in range(PARTS)]
    theirs = [swap(x, "dp", 1) for x in mine]
    codes, sums = [], []
    for k in range(PARTS):
        far = len(blocks) if k == PARTS - 1 else 1
        block, sums = decode(mine[k], theirs[k], b_enc, w_dec, k * part, sums, far)
        codes.append(block)
    codes_t = turn(*codes)
    total, near = reduce_rows(sums)
    factor = 0.1 / 0.9 / codes_t.shape[1]
    err = spread(error(total, near, rows, factor))
    return adam(codes_t, err, dec_m, dec_v)


def solution(mesh):
    in_specs = (
        P(("groups", "latent", "dp"), None),
        P(("groups", "dp"), "latent"),
        P(("groups", "latent")),
        P(("groups", "latent"), "dp"),
        P(("groups", "latent"), "dp"),
        P(("groups", "latent"), "dp"),
    )
    out_specs = P(("groups", "latent"), "dp")
    return jax.shard_map(
        per_device, mesh=mesh, in_specs=in_specs, out_specs=out_specs, check_vma=False
    )
```

```python
import functools

import jax
import jax.numpy as jnp
from jax import lax
from jax.experimental import pallas as pl
from jax.experimental.pallas import tpu as pltpu
from jax.sharding import PartitionSpec as P

MIB = 1 << 20
PARTS = 2
WHOLE = pl.BlockSpec(memory_space=pltpu.VMEM)
DIRECT = 8


def swap(value, axis, mask):
    n = lax.axis_size(axis)
    return lax.ppermute(value, axis, [(i, i ^ mask) for i in range(n)])


def params(mib):
    return pltpu.CompilerParams(vmem_limit_bytes=mib * MIB)


def waits(mib):
    return pl.CostEstimate(flops=mib * 350_000_000, bytes_accessed=mib * MIB, transcendentals=0)


def resident(value):
    return pltpu.with_memory_space_constraint(value, pltpu.VMEM)


def far_masks():
    return range(2, lax.axis_size("latent"), 2)


def stack(refs):
    return jnp.concatenate([r[...].astype(jnp.float32) for r in refs]).astype(refs[0].dtype)


def near_kernel(*refs):
    *rows, out = refs
    half = out.shape[1]
    side = lax.axis_index("dp")

    def write(order, at):
        picked = [rows[i][:, at : at + half].astype(jnp.float32) for i in order]
        out[...] = jnp.concatenate(picked).astype(out.dtype)

    pairs = range(0, len(rows), 2)

    @pl.when(side == 0)
    def _():
        write([i + c for i in pairs for c in (0, 1)], 0)

    @pl.when(side == 1)
    def _():
        write([i + c for i in pairs for c in (1, 0)], half)


def copy_kernel(x, out):
    out[...] = x[...]


def near_rows(acts, near):
    axes = ("latent", "dp")
    own = pl.pallas_call(
        copy_kernel,
        out_shape=jax.ShapeDtypeStruct(acts.shape, acts.dtype),
        in_specs=[WHOLE],
        out_specs=WHOLE,
        cost_estimate=waits(1),
        compiler_params=params(4),
    )(acts)
    rows = [own] + [swap(acts, axes, mask) for mask in range(1, 2 * near)]
    return pl.pallas_call(
        near_kernel,
        out_shape=jax.ShapeDtypeStruct((len(rows) * acts.shape[0], acts.shape[1] // 2), acts.dtype),
        in_specs=[WHOLE] * len(rows),
        out_specs=WHOLE,
        cost_estimate=waits(14),
        compiler_params=params(4),
    )(*rows)


def spread(block):
    if lax.axis_size("latent") > DIRECT:
        return [lax.all_gather(block, "latent", axis=0, tiled=True)]
    return [block] + [swap(block, "latent", mask) for mask in far_masks()]


def encode_kernel(first, *refs):
    *rows_refs, w, out = refs
    lat = out.shape[1]
    out[...] = jnp.dot(
        stack(rows_refs), w[:, first : first + lat], preferred_element_type=jnp.float32
    )


def encode(blocks, w_enc, first, lat):
    tokens = sum(b.shape[0] for b in blocks)
    return pl.pallas_call(
        functools.partial(encode_kernel, first),
        out_shape=jax.ShapeDtypeStruct((tokens, lat), jnp.float32),
        in_specs=[WHOLE] * (len(blocks) + 1),
        out_specs=WHOLE,
        cost_estimate=waits(7),
        compiler_params=params(8),
    )(*blocks, resident(w_enc))


def decode_kernel(first, given, mine, theirs, bias, w, *refs):
    codes, *out = refs[given:]
    lat = mine.shape[1]
    pre = mine[...] + theirs[...] + bias[:, first : first + lat]
    block = jnp.maximum(pre, 0.0).astype(jnp.bfloat16)
    codes[...] = block
    total = jnp.dot(block, w[first : first + lat, :], preferred_element_type=jnp.float32)
    if given:
        total = total + refs[0][...]
    rows = out[0].shape[0]
    for j, ref in enumerate(out):
        ref[...] = total[j * rows : (j + 1) * rows].astype(ref.dtype)


def decode(mine, theirs, bias, w_dec, first, given, far):
    tokens, lat = mine.shape
    half = w_dec.shape[1]
    sums = [
        jax.ShapeDtypeStruct((tokens // far, half), jnp.bfloat16 if j else jnp.float32)
        for j in range(far)
    ]
    codes, *sums = pl.pallas_call(
        functools.partial(decode_kernel, first, len(given)),
        out_shape=[jax.ShapeDtypeStruct((tokens, lat), jnp.bfloat16)] + sums,
        in_specs=[WHOLE] * (4 + len(given)),
        out_specs=[WHOLE] * (1 + len(sums)),
        cost_estimate=waits(7),
        compiler_params=params(8),
    )(mine, theirs, bias.reshape(1, -1), resident(w_dec), *given)
    return codes, sums


def turn_kernel(chunk, *refs):
    *codes, out = refs
    for k, ref in enumerate(codes):
        lat = ref.shape[1]

        @pl.loop(0, lat // chunk)
        def _(i):
            at = pl.multiple_of(i * chunk, chunk)
            block = ref[:, pl.ds(at, chunk)].astype(jnp.float32).T
            out[pl.ds(k * lat + at, chunk), :] = block.astype(out.dtype)


def turn(*codes):
    tokens, lat = codes[0].shape
    return pl.pallas_call(
        functools.partial(turn_kernel, min(512, lat)),
        out_shape=jax.ShapeDtypeStruct((len(codes) * lat, tokens), codes[0].dtype),
        in_specs=[WHOLE] * len(codes),
        out_specs=WHOLE,
        cost_estimate=waits(4),
        compiler_params=params(8),
    )(*codes)


def sum_kernel(own, *refs):
    *terms, out = refs
    total = own[...]
    for ref in terms:
        total = total + ref[...]
    out[...] = total


def add_up(terms):
    return pl.pallas_call(
        sum_kernel,
        out_shape=jax.ShapeDtypeStruct(terms[0].shape, jnp.float32),
        in_specs=[WHOLE] * len(terms),
        out_specs=WHOLE,
        cost_estimate=waits(8),
        compiler_params=params(4),
    )(*terms)


def error_kernel(factor, total, rows, *refs):
    *near, out = refs
    total = total[...]
    for ref in near:
        half = ref.shape[0] // 2
        total = total + jnp.concatenate([ref[half:], ref[:half]])
    out[...] = ((total - rows[...].astype(jnp.float32)) * factor).astype(out.dtype)


def error(total, near, rows, factor):
    return pl.pallas_call(
        functools.partial(error_kernel, factor),
        out_shape=jax.ShapeDtypeStruct(rows.shape, rows.dtype),
        in_specs=[WHOLE] * (2 + len(near)),
        out_specs=WHOLE,
        cost_estimate=waits(8),
        compiler_params=params(4),
    )(total, rows, *near)


def reduce_rows(sums):
    if lax.axis_size("latent") > DIRECT:
        return lax.psum_scatter(sums[0], "latent", scatter_dimension=0, tiled=True), []
    terms = [sums[0]] + [swap(s, "latent", mask) for s, mask in zip(sums[1:], far_masks())]
    total = add_up(terms)
    return total, [swap(total, "latent", 1)]


def adam_kernel(codes_t, m, v, *refs):
    *blocks, out, even, odd, err = refs
    products = (even, odd)
    b1, b2 = 1.0 - 0.9**10, 1.0 - 0.999**10
    p = 0.999 / 0.081
    scale = 0.9 / b1 / (0.081 / b2) ** 0.5
    eps = 1e-8 / (0.9 / b1) * scale**2
    p, scale, eps = (jnp.asarray(x, out.dtype) for x in (p, scale, eps))
    i, last = pl.program_id(0), pl.num_programs(0) - 1
    rows = out.shape[0]
    part = even.shape[0]
    slab = 16

    def multiply(start, product):
        at = pl.ds(pl.multiple_of(start, part), part)
        c = jnp.dot(codes_t[at, :], err[...], preferred_element_type=jnp.float32)
        product[...] = c.astype(product.dtype)

    @pl.when(i == 0)
    def _():
        err[...] = stack(blocks)
        multiply(0, even)

    for k in range(2):
        if k == 0:
            multiply(i * rows + part, odd)
        else:
            multiply(jnp.minimum(i + 1, last) * rows, even)
        for r in range(0, part, slab):
            at = pl.ds(pl.multiple_of(i * rows + k * part + r, slab), slab)
            c = products[k][r : r + slab, :]
            first = m[at, :] + c
            second = v[at, :] * p + c * c
            inverse = lax.rsqrt(second)
            step = first * (inverse * (scale - inverse * eps))
            out[k * part + r : k * part + r + slab, :] = step


def adam(codes_t, blocks, m, v):
    lat, half = m.shape
    rows = min(512, lat)
    return pl.pallas_call(
        adam_kernel,
        grid=(lat // rows,),
        out_shape=jax.ShapeDtypeStruct(m.shape, jnp.bfloat16),
        in_specs=[WHOLE] * (3 + len(blocks)),
        out_specs=pl.BlockSpec((rows, half), lambda i: (i, 0)),
        scratch_shapes=[pltpu.VMEM((rows // 2, half), jnp.bfloat16)] * 2
        + [pltpu.VMEM((codes_t.shape[1], half), jnp.bfloat16)],
        compiler_params=params(12),
    )(codes_t, resident(m), resident(v), *blocks)


def per_device(acts, w_enc, b_enc, w_dec, dec_m, dec_v):
    direct = lax.axis_size("latent") <= DIRECT
    rows = near_rows(acts, 2 if direct else 1)
    blocks = spread(rows)
    part = w_enc.shape[1] // PARTS
    mine = [encode(blocks, w_enc, k * part, part) for k in range(PARTS)]
    theirs = [swap(x, "dp", 1) for x in mine]
    codes, sums = [], []
    for k in range(PARTS):
        far = len(blocks) if k == PARTS - 1 else 1
        block, sums = decode(mine[k], theirs[k], b_enc, w_dec, k * part, sums, far)
        codes.append(block)
    codes_t = turn(*codes)
    total, near = reduce_rows(sums)
    factor = 0.1 / 0.9 / codes_t.shape[1]
    err = spread(error(total, near, rows, factor))
    return adam(codes_t, err, dec_m, dec_v)


def solution(mesh):
    in_specs = (
        P(("groups", "latent", "dp"), None),
        P(("groups", "dp"), "latent"),
        P(("groups", "latent")),
        P(("groups", "latent"), "dp"),
        P(("groups", "latent"), "dp"),
        P(("groups", "latent"), "dp"),
    )
    out_specs = P(("groups", "latent"), "dp")
    return jax.shard_map(
        per_device, mesh=mesh, in_specs=in_specs, out_specs=out_specs, check_vma=False
    )
```
